32 devices in a mesh: groups: 2 (over y), expert: 8 (over z, x), tensor: 2 (over core).
Axes of the slice: x: 2, y: 2, z: 4, core: 2. Of those that a mesh axis runs over, the one named last changes fastest.
Arguments:
- tokens: bfloat16 [1024, 3584], P(('groups', 'expert')), parts along dimension 0, may hold values from -6 to 6
- expert_ids: int32 [1024, 2], P(('groups', 'expert')), parts along dimension 0, may hold values from 0 to 27, all different within a row; in each aligned block of 64 rows (0 to 63, 64 to 127, ...) at most 5 rows name the same one
- route_weights: float32 [1024, 2], P(('groups', 'expert')), parts along dimension 0, may hold values from 0.05 to 0.5
- slot_plan: int32 [64], P('groups'), parts along dimension 0, may hold values from 0 to 27, as said below
- w_gate: bfloat16 [256, 3584, 256], P(('groups', 'expert'), None, 'tensor'), parts along dimension 0, as said below
- w_up: bfloat16 [256, 3584, 256], P(('groups', 'expert'), None, 'tensor'), parts along dimension 0, as said below
- w_down: bfloat16 [256, 256, 3584], P(('groups', 'expert'), 'tensor'), parts along dimension 0, as said below
Outputs:
- mixed: bfloat16 [1024, 3584], P(('groups', 'expert'), 'tensor'), parts along dimension 0
The draws below stay inside these ranges and needn't reach their ends.
There are 2 independent parts, one for each index of `groups`. The reference program is written for one: setup_inputs(seed, part) draws one part's arguments, and reference() takes and returns one part's arrays. A program takes and returns all parts, laid end to end along the dimension named above; each array names one. Nothing has to cross between parts.
Inputs may be any that keep to these rules, and one draw needn't show every extreme that they name: `expert_ids`: within the rows of one device (aligned blocks of 64 tokens) no expert is named more than 5 times; a token names 2 different experts. `slot_plan`: every expert is hosted by one slot, and exactly 4 experts by two. `w_gate`: slots that host the same expert hold equal blocks. `w_up`: slots that host the same expert hold equal blocks. `w_down`: slots that host the same expert hold equal blocks.
All inputs are finite; a program needn't handle non-finite values.
Results may differ from the reference program's by a relative error of at most 0.0065.
Values may be sent and summed in bfloat16 or wider, within the bound.
No kernel may reach another device: no remote copies, remote signals or barrier semaphores. Data moves between devices by JAX's collectives and lax.ppermute only.
A program may use at most 128 MiB of HBM per device.

```python
import math
import jax
import jax.numpy as jnp
import numpy as np
from jax import lax

D = 3584
UNIT = 128
HB = 4
EXPERT_HID = 1024
SLOTS = 32
SPARES = 4
EXPERTS = 28
TOP = 2
TOK_DEV = 64
CAP = 5
TOKENS = 512
N_EXPERT = 8


def plan_of(key):
    first_key, second_key = jax.random.split(jax.random.fold_in(key, 11))
    hot = jax.random.permutation(first_key, EXPERTS)[:SPARES].astype(jnp.int32)
    listed = jnp.concatenate([jnp.arange(EXPERTS, dtype=jnp.int32), hot])
    order = jax.random.permutation(second_key, SLOTS)
    return listed[order].astype(jnp.int32)


def draw_slot_plan(key, part):
    return plan_of(key)


def draw_w_gate(key, part):
    plan = plan_of(key)
    key = jax.random.fold_in(key, 2)
    base = jax.random.normal(key, (EXPERTS, HB, D, 2 * UNIT), jnp.float32)
    return (base[plan] * D ** (-0.5)).reshape(SLOTS * HB, D, 2 * UNIT).astype(jnp.bfloat16)


def draw_w_up(key, part):
    plan = plan_of(key)
    key = jax.random.fold_in(key, 3)
    base = jax.random.normal(key, (EXPERTS, HB, D, 2 * UNIT), jnp.float32)
    return (base[plan] * D ** (-0.5)).reshape(SLOTS * HB, D, 2 * UNIT).astype(jnp.bfloat16)


def draw_w_down(key, part):
    plan = plan_of(key)
    key = jax.random.fold_in(key, 4)
    base = jax.random.normal(key, (EXPERTS, HB, 2 * UNIT, D), jnp.float32)
    return (base[plan] * EXPERT_HID ** (-0.5)).reshape(SLOTS * HB, 2 * UNIT, D).astype(jnp.bfloat16)


def levels(rng, extent, cuts, low, top_value):
    factor_of, own = 1.0, jax.random.fold_in(rng, 6)
    for position, blocks in cuts:
        heights = jnp.exp(jax.random.uniform(jax.random.fold_in(own, position), (blocks,), jnp.float32, low / len(cuts), top_value / len(cuts)))
        factor_of = factor_of * jnp.repeat(heights, extent[position] // blocks).reshape([-1 if axis == position else 1 for axis in range(len(extent))])
    return factor_of


def routed_block(own_key, own, number, rows, number_of, top, bound, slope):
    order = jax.random.permutation(own_key, number_of)
    crowded, ordinary = shares(number_of, rows * top, bound, slope, True), shares(number_of, rows * top, bound, slope, False)
    places = jnp.arange(number_of)

    def named(tallies, turn):
        used = int((tallies > 0).sum())
        fixed = max(1, used // 4)
        moved = fixed + (places - fixed + turn * (used - fixed)) % max(1, number_of - fixed)
        return jnp.zeros((number_of,), jnp.int32).at[order[jnp.where(places < fixed, places, moved)]].set(jnp.asarray(tallies, jnp.int32))

    tallies = jnp.where(number % 4 == 0, named(crowded, number // 4), named(ordinary, number - number // 4 - 1))
    mixed = jax.random.permutation(jax.random.fold_in(own, 3), number_of)
    donor, sink = mixed[0:number_of // 2 * 2:2], mixed[1:number_of // 2 * 2:2]
    margin = jnp.minimum(tallies[donor] - 1, bound - tallies[sink]) // 2
    margin = jnp.where((donor == order[0]) | (sink == order[0]) | (tallies[sink] == 0), 0, jnp.maximum(margin, 0))
    moved = jax.random.randint(jax.random.fold_in(own, 4), (number_of // 2,), 0, 1 << 20) % (margin + 1)
    tallies = tallies.at[donor].add(-moved).at[sink].add(moved)
    labels = jnp.searchsorted(jnp.cumsum(tallies), jnp.arange(rows * top), side="right").astype(jnp.int32)
    listing = labels.reshape(top, rows).T
    listing = listing[jax.random.permutation(jax.random.fold_in(own, 1), rows)]
    turn = jax.random.randint(jax.random.fold_in(own, 2), (rows, 1), 0, top)
    return jnp.take_along_axis(listing, (jnp.arange(top)[None, :] + turn) % top, axis=1)


def shares(number_of, total, most, slope, full):
    loads = [(1 << 20) // math.isqrt(standing ** slope) + 1 for standing in range(1, number_of + 1)]
    largest = most if full else min(most, max(-(-total // number_of), total * loads[0] // sum(loads)))
    least = 1 if total - largest >= number_of - 1 else 0
    given, rest = [largest] + [least] * (number_of - 1), total - largest - least * (number_of - 1)
    while rest > 0:
        movable = [i for i in range(1, number_of) if given[i] < largest] or [i for i in range(1, number_of) if given[i] < most]
        pool, left = sum([loads[i] for i in movable]), rest
        for i in movable:
            extra = min(most - given[i], max(1, left * loads[i] // pool), rest)
            given[i] = given[i] + extra
            rest = rest - extra
    return np.array(given)


def normal_values(key, dims, width, bound, pieces=(), held_as=jnp.bfloat16):
    loudness = levels(key, dims, pieces, -0.22, 0.18) if pieces else 1.0
    entries = jax.random.normal(key, dims, jnp.float32) * width * loudness
    return jnp.minimum(jnp.maximum(entries, -bound), bound).astype(held_as)


def setup_inputs(seed: int = 0, part: int = 0) -> dict:
    keys = jax.random.split(jax.random.key(seed), 8)
    part_splits = jax.random.split(jax.random.fold_in(keys[7], part), 8)
    tokens = normal_values(part_splits[0], (TOKENS, D), 1.0, 6.0, ((0, 8),))
    expert_ids_keys = jax.random.split(jax.random.fold_in(part_splits[1], 1), TOKENS // TOK_DEV)
    expert_ids_turns = jax.random.permutation(jax.random.fold_in(part_splits[1], 3), TOKENS // TOK_DEV)
    expert_ids = jax.vmap(lambda own, number: routed_block(jax.random.fold_in(part_splits[1], 2), own, number, TOK_DEV, EXPERTS, TOP, CAP, 2))(expert_ids_keys, expert_ids_turns).reshape((TOKENS, TOP))
    route_weights = jnp.clip(0.05 + 0.45 * jax.random.uniform(part_splits[2], (TOKENS, TOP), jnp.float32) ** levels(part_splits[2], (TOKENS, TOP), ((0, 8),), -0.2, 0.2), 0.05, 0.5)
    slot_plan = draw_slot_plan(jax.random.fold_in(jax.random.fold_in(keys[7], part), 71), part)
    w_gate = draw_w_gate(jax.random.fold_in(jax.random.fold_in(keys[7], part), 71), part)
    w_up = draw_w_up(jax.random.fold_in(jax.random.fold_in(keys[7], part), 71), part)
    w_down = draw_w_down(jax.random.fold_in(jax.random.fold_in(keys[7], part), 71), part)
    return dict(tokens=tokens, expert_ids=expert_ids, route_weights=route_weights, slot_plan=slot_plan, w_gate=w_gate, w_up=w_up, w_down=w_down)


def reference(tokens, expert_ids, route_weights, slot_plan, w_gate, w_up, w_down):
    slot_iota = jnp.arange(SLOTS, dtype=jnp.int32)
    expert_iota = jnp.arange(EXPERTS, dtype=jnp.int32)
    hosted = slot_plan[None, :] == expert_iota[:, None]
    first_slot = jnp.min(jnp.where(hosted, slot_iota[None, :], SLOTS), axis=1).astype(jnp.int32)
    gate_all = w_gate.reshape(SLOTS, HB, D, 2 * UNIT)
    up_all = w_up.reshape(SLOTS, HB, D, 2 * UNIT)
    down_all = w_down.reshape(SLOTS, HB, 2, UNIT, D)
    flat_ids = expert_ids.reshape(-1)
    flat_weights = route_weights.reshape(-1)
    row_limit = CAP * N_EXPERT

    def one_expert(total, expert):
        slot = first_slot[expert]
        gate_w = gate_all[slot].astype(jnp.float32)
        up_w = up_all[slot].astype(jnp.float32)
        down_w = down_all[slot].astype(jnp.float32)
        naming = flat_ids == expert
        picked = jnp.nonzero(naming, size=row_limit, fill_value=0)[0].astype(jnp.int32)
        count = jnp.sum(naming.astype(jnp.int32))
        live = (jnp.arange(row_limit, dtype=jnp.int32) < count).astype(jnp.float32)
        token_index = (picked // TOP).astype(jnp.int32)
        rows = tokens[token_index].astype(jnp.float32)
        gate = jnp.einsum("rd,bdu->rbu", rows, gate_w, precision=lax.Precision.HIGHEST)
        upper = jnp.einsum("rd,bdu->rbu", rows, up_w, precision=lax.Precision.HIGHEST)
        hidden = lax.optimization_barrier((jax.nn.silu(gate) * upper).astype(jnp.bfloat16))
        halves = hidden.reshape(row_limit, HB, 2, UNIT).astype(jnp.float32)
        unit_out = jnp.einsum("rbcu,bcud->rbcd", halves, down_w, precision=lax.Precision.HIGHEST)
        unit_out = lax.optimization_barrier(unit_out.astype(jnp.bfloat16)).astype(jnp.float32)
        block_out = lax.optimization_barrier((unit_out[:, :, 0] + unit_out[:, :, 1]).astype(jnp.bfloat16))
        merged = jnp.sum(block_out.astype(jnp.float32), axis=1) * (flat_weights[picked] * live)[:, None]
        return total.at[token_index].add(merged), None

    total, _ = lax.scan(one_expert, jnp.zeros((TOKENS, D), jnp.float32), expert_iota)
    return total.astype(jnp.bfloat16)
```

```python
import functools
import jax
import jax.numpy as jnp
import numpy as np
from jax import lax
from jax.experimental import pallas as pl
from jax.experimental.pallas import tpu as pltpu
from jax.sharding import PartitionSpec as P

HB = 4
SLOTS = 32
EXPERTS = 28
CAP = 5
STEP_BLOCKS = 2
MIB = 1 << 20


def swapped(shard, axis, stride):
    return lax.ppermute(shard, axis, [(i, i ^ 1 << stride) for i in range(lax.axis_size(axis))])


def shards(tokens, expert_ids, route_weights, slot_plan, w_gate, w_up, w_down):
    devices = lax.axis_size("expert")
    core = lax.axis_index("tensor")
    blocks_dev = w_gate.shape[0]
    slots_dev = max(1, blocks_dev // HB)
    width = tokens.shape[1]
    half = width // 2
    tok_rows = tokens.shape[0]
    picks_tok = expert_ids.shape[1]
    flat_ids = expert_ids.reshape(-1)
    slot_iota = jnp.arange(SLOTS, dtype=jnp.int32)
    expert_iota = jnp.arange(EXPERTS, dtype=jnp.int32)
    hosted = slot_plan[None, :] == expert_iota[:, None]
    first_slot = jnp.min(jnp.where(hosted, slot_iota[None, :], SLOTS), axis=1)
    naming = (flat_ids[:, None] == expert_iota[None, :]).astype(jnp.int32)
    lowest = jnp.sum(naming * first_slot[None, :], axis=1)
    placed = (lowest[:, None] == slot_iota[None, :]).astype(jnp.int32)
    position = jnp.sum((jnp.cumsum(placed, axis=0) - placed) * placed, axis=1)
    entry_iota = np.arange(devices * slots_dev)
    dest_slot = jnp.asarray(
        entry_iota // slots_dev * blocks_dev // HB + entry_iota % slots_dev, jnp.int32
    )
    slot_match = dest_slot[:, None] == lowest[None, :]
    row_match = jnp.arange(CAP, dtype=jnp.int32)[:, None] == position[None, :]
    routing = (slot_match[:, None, :] & row_match[None, :, :]).astype(jnp.int32)
    routing = routing.reshape(devices * slots_dev * CAP, tok_rows, picks_tok)
    tok_iota = jnp.arange(tok_rows, dtype=jnp.int32)
    source_row = jnp.sum(routing * tok_iota[None, :, None], axis=(1, 2))
    live_row = jnp.sum(routing, axis=(1, 2)) > 0
    block_slot = np.arange(blocks_dev) // HB
    outgoing = jnp.where(live_row[:, None], tokens[source_row], jnp.zeros((), jnp.bfloat16))
    outgoing = outgoing.reshape(devices, slots_dev, CAP, width)
    picked = jnp.take(
        lax.all_to_all(outgoing, "expert", split_axis=0, concat_axis=0, tiled=True),
        block_slot,
        axis=1,
    )
    gate = jnp.einsum("nbcd,bdu->nbcu", picked, w_gate, preferred_element_type=jnp.float32)
    upper = jnp.einsum("nbcd,bdu->nbcu", picked, w_up, preferred_element_type=jnp.float32)
    hidden = (jax.nn.silu(gate) * upper).astype(jnp.bfloat16)
    result = jnp.einsum("nbcu,bud->nbcd", hidden, w_down, preferred_element_type=jnp.float32)
    result = lax.optimization_barrier(result.astype(jnp.bfloat16))
    mine = lax.dynamic_slice_in_dim(result, core * half, half, 3)
    other = lax.dynamic_slice_in_dim(result, (1 - core) * half, half, 3)
    partner = swapped(other, "tensor", 0)
    outputs = (mine.astype(jnp.float32) + partner.astype(jnp.float32)).astype(jnp.bfloat16)
    returned = lax.all_to_all(outputs, "expert", split_axis=0, concat_axis=0, tiled=True)
    returned = returned.reshape(-1, half)
    block_iota = jnp.arange(HB, dtype=jnp.int32)
    row_index = (lowest[:, None] * HB + block_iota[None, :]) * CAP + position[:, None]
    gathered = returned[row_index.reshape(-1)].reshape(tok_rows, picks_tok, HB, half)
    summed = jnp.sum(gathered.astype(jnp.float32), axis=2)
    mixed = jnp.sum(summed * route_weights[:, :, None], axis=1)
    return mixed.astype(jnp.bfloat16)


def quotient(values, divisor):
    return lax.shift_right_logical(values * ((1 << 16) // divisor + 1), 16)


def iota(shape, axis):
    return lax.broadcasted_iota(jnp.int32, shape, axis)


def column(row):
    size = row.shape[1]
    eye = iota((size, size), 0) == iota((size, size), 1)
    return jnp.sum(jnp.where(eye, row, jnp.zeros((), row.dtype)), axis=1, keepdims=True)


def onehot(mask):
    return jnp.where(mask, 1.0, 0.0).astype(jnp.bfloat16)


def dot(left, right, over=1):
    dims = (((over,), (0,)), ((), ()))
    return lax.dot_general(left, right, dims, preferred_element_type=jnp.float32)


def pick_kernel(slots_dev, key_ref, ids_ref, plan_ref, tok_ref, pick_ref, *send_refs):
    rounds = len(send_refs)
    rows = slots_dev * CAP
    packed = 2 * rows * rounds
    tok_rows, width = tok_ref.shape
    half = width // 2
    slots = plan_ref.shape[1]
    plan = plan_ref[...]
    earlier = (column(plan) == plan) & (iota((slots, slots), 0) < iota((slots, slots), 1))
    repeated = jnp.sum(jnp.where(earlier, 1, 0), axis=0, keepdims=True) > 0
    served = jnp.where(repeated, -1, plan)

    index = iota((packed, 1), 0)
    part = quotient(index, rows)
    entry = quotient(index, CAP)
    rank = index - entry * CAP
    slot = (key_ref[0] ^ lax.shift_right_logical(part, 1)) * slots_dev + entry - part * slots_dev
    side = part & 1
    chosen = jnp.where(iota((packed, slots), 1) == slot, served, 0)
    expert = jnp.sum(chosen, axis=1, keepdims=True)

    ids = jnp.concatenate([ids_ref[...], ids_ref[...]], axis=1)
    lanes = 2 * tok_rows
    lane = iota((packed, lanes), 1)
    same_side = jnp.where(lane < tok_rows, 0, 1) == side
    named = [(expert == ids[k : k + 1, :]) & same_side for k in range(ids.shape[0])]
    either = functools.reduce(jnp.logical_or, named)
    before = onehot(iota((lanes, lanes), 0) < iota((lanes, lanes), 1))
    in_row = dot(onehot(either), before) == rank.astype(jnp.float32)
    for k, mask in enumerate(named):
        pick_ref[k, :, :] = onehot(mask & in_row)
    stacked = jnp.concatenate([tok_ref[:, :half], tok_ref[:, half:]], axis=0)
    sent = dot(onehot(either & in_row), stacked).astype(jnp.bfloat16)
    for p, send_ref in enumerate(send_refs):
        send_ref[...] = sent[2 * rows * p : 2 * rows * (p + 1), :]


def expert_kernel(slots_dev, bufs, *refs):
    buf_refs = refs[:bufs]
    gate_ref, up_ref, down_ref, mine_ref, other_ref, x_ref, acc_ref = refs[bufs:]
    rows = slots_dev * CAP
    total = bufs * rows
    half = buf_refs[0].shape[1]
    step = pl.program_id(0)

    @pl.when(step == 0)
    def _():
        got = jnp.concatenate([ref[...] for ref in buf_refs], axis=0)
        place = iota((total, 2 * total), 0)
        place = place + rows * quotient(place, rows)
        lane = iota((total, 2 * total), 1)
        x_ref[:, :half] = dot(onehot(lane == place), got).astype(jnp.bfloat16)
        x_ref[:, half:] = dot(onehot(lane == place + rows), got).astype(jnp.bfloat16)
        acc_ref[...] = jnp.zeros_like(acc_ref)

    x = x_ref[...]
    index = iota((total, 1), 0)
    row_slot = quotient(index, CAP) - quotient(index, rows) * slots_dev
    hidden = []
    for b in range(STEP_BLOCKS):
        both = dot(x, jnp.concatenate([gate_ref[b], up_ref[b]], axis=1))
        unit = gate_ref.shape[2]
        gate, upper = both[:, :unit], both[:, unit:]
        value = gate / (1.0 + jnp.exp(-gate)) * upper
        mine = row_slot == (step * STEP_BLOCKS + b) // HB
        hidden.append(jnp.where(mine, value, 0.0).astype(jnp.bfloat16))
    down = jnp.concatenate([down_ref[b] for b in range(STEP_BLOCKS)], axis=0)
    acc_ref[...] += dot(jnp.concatenate(hidden, axis=1), down)

    @pl.when(step == pl.num_programs(0) - 1)
    def _():
        mine_ref[...] = acc_ref[: total // 2, :]
        other_ref[...] = acc_ref[total // 2 :, :].astype(jnp.bfloat16)


def sum_kernel(rows, mine_ref, got_ref, *send_refs):
    total = mine_ref.shape[0]
    half = mine_ref.shape[1] // 2
    summed = (mine_ref[...] + got_ref[...].astype(jnp.float32)).astype(jnp.bfloat16)
    stacked = jnp.concatenate([summed[:, :half], summed[:, half:]], axis=0)
    index = iota((2 * total, 2 * total), 0)
    part = quotient(index, rows)
    source = index - rows * part + rows * lax.shift_right_logical(part, 1) + total * (part & 1)
    packed = dot(onehot(iota((2 * total, 2 * total), 1) == source), stacked).astype(jnp.bfloat16)
    for p, send_ref in enumerate(send_refs):
        send_ref[...] = packed[2 * rows * p : 2 * rows * (p + 1), :]


def combine_kernel(bufs, core_ref, pick_ref, weight_ref, *refs):
    got = jnp.concatenate([ref[...] for ref in refs[:bufs]], axis=0)
    keep_ref, give_ref, sum_ref = refs[bufs:]
    tok_rows = keep_ref.shape[0]
    mixed = None
    for k in range(pick_ref.shape[0]):
        weight = column(weight_ref[k : k + 1, :])
        term = dot(pick_ref[k], got, 0) * jnp.concatenate([weight, weight], axis=0)
        mixed = term if mixed is None else mixed + term
    sum_ref[...] = mixed
    core = core_ref[0]
    keep_ref[...] = sum_ref[pl.ds(pl.multiple_of(core * tok_rows, 8), tok_rows), :]
    give_ref[...] = sum_ref[pl.ds(pl.multiple_of((1 - core) * tok_rows, 8), tok_rows), :].astype(jnp.bfloat16)


VMEM = pl.BlockSpec(memory_space=pltpu.VMEM)
SMEM = pl.BlockSpec(memory_space=pltpu.SMEM)


def params(mib):
    return pltpu.CompilerParams(vmem_limit_bytes=mib * MIB)


def shards_paired(tokens, expert_ids, route_weights, slot_plan, w_gate, w_up, w_down):
    chips = lax.axis_size("expert")
    rounds = chips // 2
    core = lax.axis_index("tensor").astype(jnp.int32)
    chip = lax.axis_index("expert").astype(jnp.int32)
    slots_dev = w_gate.shape[0] // HB
    rows = slots_dev * CAP
    tok_rows, width = tokens.shape
    half = width // 2
    picks = expert_ids.shape[1]
    packed = jax.ShapeDtypeStruct((2 * rows, half), jnp.bfloat16)
    key = (chip ^ (core * rounds)).reshape(1)

    def travel(arrays):
        return [
            lax.ppermute(
                array,
                ("expert", "tensor"),
                [(2 * i + c, 2 * (i ^ (p + rounds * c)) + c) for i in range(chips) for c in range(2)],
            )
            for p, array in enumerate(arrays)
        ]

    pick, *sent = pl.pallas_call(
        functools.partial(pick_kernel, slots_dev),
        out_shape=[jax.ShapeDtypeStruct((picks, 2 * rows * rounds, 2 * tok_rows), jnp.bfloat16)] + [packed] * rounds,
        in_specs=[SMEM, VMEM, VMEM, VMEM],
        out_specs=[VMEM] * (1 + rounds),
        compiler_params=params(16),
        name="pick_rows",
    )(key, expert_ids.T, slot_plan.reshape(1, -1), tokens)

    got = travel(sent)
    got = got + [swapped(array, "tensor", 0) for array in got]

    total = chips * rows
    blocks, _, unit = w_gate.shape
    whole = lambda shape: pl.BlockSpec(shape, lambda i: (0, 0))
    mine, other = pl.pallas_call(
        functools.partial(expert_kernel, slots_dev, chips),
        grid=(blocks // STEP_BLOCKS,),
        out_shape=[
            jax.ShapeDtypeStruct((total // 2, width), jnp.float32),
            jax.ShapeDtypeStruct((total // 2, width), jnp.bfloat16),
        ],
        in_specs=[whole((2 * rows, half))] * chips
        + [
            pl.BlockSpec((STEP_BLOCKS, width, unit), lambda i: (i, 0, 0)),
            pl.BlockSpec((STEP_BLOCKS, width, unit), lambda i: (i, 0, 0)),
            pl.BlockSpec((STEP_BLOCKS, unit, width), lambda i: (i, 0, 0)),
        ],
        out_specs=[whole((total // 2, width))] * 2,
        scratch_shapes=[
            pltpu.VMEM((total, width), jnp.bfloat16),
            pltpu.VMEM((total, width), jnp.float32),
        ],
        compiler_params=params(40),
        name="experts",
    )(*got, w_gate, w_up, w_down)

    back = pl.pallas_call(
        functools.partial(sum_kernel, rows),
        out_shape=[packed] * rounds,
        in_specs=[VMEM, VMEM],
        out_specs=[VMEM] * rounds,
        compiler_params=params(16),
        name="sum_cores",
    )(mine, swapped(other, "tensor", 0))

    home = travel(back)
    keep, give = pl.pallas_call(
        functools.partial(combine_kernel, rounds),
        out_shape=[
            jax.ShapeDtypeStruct((tok_rows, half), jnp.float32),
            jax.ShapeDtypeStruct((tok_rows, half), jnp.bfloat16),
        ],
        in_specs=[SMEM] + [VMEM] * (2 + rounds),
        out_specs=[VMEM] * 2,
        scratch_shapes=[pltpu.VMEM((2 * tok_rows, half), jnp.float32)],
        compiler_params=params(16),
        name="combine",
    )(core.reshape(1), pick, route_weights.T, *home)
    return (keep + swapped(give, "tensor", 0).astype(jnp.float32)).astype(jnp.bfloat16)


def solution(mesh):
    in_specs = (
        P(("groups", "expert"), None),
        P(("groups", "expert"), None),
        P(("groups", "expert"), None),
        P("groups"),
        P(("groups", "expert"), None, "tensor"),
        P(("groups", "expert"), None, "tensor"),
        P(("groups", "expert"), "tensor", None),
    )
    out_specs = P(("groups", "expert"), "tensor")
    chips = mesh.shape["expert"]
    paired = mesh.shape["tensor"] == 2 and chips in (2, 4, 8) and SLOTS % chips == 0
    body = shards_paired if paired else shards
    return jax.shard_map(body, mesh=mesh, in_specs=in_specs, out_specs=out_specs, check_vma=False)
```

```python
import functools
import jax
import jax.numpy as jnp
import numpy as np
from jax import lax
from jax.experimental import pallas as pl
from jax.experimental.pallas import tpu as pltpu
from jax.sharding import PartitionSpec as P

HB = 4
SLOTS = 32
EXPERTS = 28
CAP = 5
UNROLL = 8
COLUMNS = 512
LIMIT = 14
RING = 4
MIB = 1 << 20


def swapped(shard, axis, stride):
    return lax.ppermute(shard, axis, [(i, i ^ 1 << stride) for i in range(lax.axis_size(axis))])


def shards(tokens, expert_ids, route_weights, slot_plan, w_gate, w_up, w_down):
    devices = lax.axis_size("expert")
    core = lax.axis_index("tensor")
    blocks_dev = w_gate.shape[0]
    slots_dev = max(1, blocks_dev // HB)
    width = tokens.shape[1]
    half = width // 2
    tok_rows = tokens.shape[0]
    picks_tok = expert_ids.shape[1]
    flat_ids = expert_ids.reshape(-1)
    slot_iota = jnp.arange(SLOTS, dtype=jnp.int32)
    expert_iota = jnp.arange(EXPERTS, dtype=jnp.int32)
    hosted = slot_plan[None, :] == expert_iota[:, None]
    first_slot = jnp.min(jnp.where(hosted, slot_iota[None, :], SLOTS), axis=1)
    naming = (flat_ids[:, None] == expert_iota[None, :]).astype(jnp.int32)
    lowest = jnp.sum(naming * first_slot[None, :], axis=1)
    placed = (lowest[:, None] == slot_iota[None, :]).astype(jnp.int32)
    position = jnp.sum((jnp.cumsum(placed, axis=0) - placed) * placed, axis=1)
    entry_iota = np.arange(devices * slots_dev)
    dest_slot = jnp.asarray(
        entry_iota // slots_dev * blocks_dev // HB + entry_iota % slots_dev, jnp.int32
    )
    slot_match = dest_slot[:, None] == lowest[None, :]
    row_match = jnp.arange(CAP, dtype=jnp.int32)[:, None] == position[None, :]
    routing = (slot_match[:, None, :] & row_match[None, :, :]).astype(jnp.int32)
    routing = routing.reshape(devices * slots_dev * CAP, tok_rows, picks_tok)
    tok_iota = jnp.arange(tok_rows, dtype=jnp.int32)
    source_row = jnp.sum(routing * tok_iota[None, :, None], axis=(1, 2))
    live_row = jnp.sum(routing, axis=(1, 2)) > 0
    block_slot = np.arange(blocks_dev) // HB
    outgoing = jnp.where(live_row[:, None], tokens[source_row], jnp.zeros((), jnp.bfloat16))
    outgoing = outgoing.reshape(devices, slots_dev, CAP, width)
    picked = jnp.take(
        lax.all_to_all(outgoing, "expert", split_axis=0, concat_axis=0, tiled=True),
        block_slot,
        axis=1,
    )
    gate = jnp.einsum("nbcd,bdu->nbcu", picked, w_gate, preferred_element_type=jnp.float32)
    upper = jnp.einsum("nbcd,bdu->nbcu", picked, w_up, preferred_element_type=jnp.float32)
    hidden = (jax.nn.silu(gate) * upper).astype(jnp.bfloat16)
    result = jnp.einsum("nbcu,bud->nbcd", hidden, w_down, preferred_element_type=jnp.float32)
    result = lax.optimization_barrier(result.astype(jnp.bfloat16))
    mine = lax.dynamic_slice_in_dim(result, core * half, half, 3)
    other = lax.dynamic_slice_in_dim(result, (1 - core) * half, half, 3)
    partner = swapped(other, "tensor", 0)
    outputs = (mine.astype(jnp.float32) + partner.astype(jnp.float32)).astype(jnp.bfloat16)
    returned = lax.all_to_all(outputs, "expert", split_axis=0, concat_axis=0, tiled=True)
    returned = returned.reshape(-1, half)
    block_iota = jnp.arange(HB, dtype=jnp.int32)
    row_index = (lowest[:, None] * HB + block_iota[None, :]) * CAP + position[:, None]
    gathered = returned[row_index.reshape(-1)].reshape(tok_rows, picks_tok, HB, half)
    summed = jnp.sum(gathered.astype(jnp.float32), axis=2)
    mixed = jnp.sum(summed * route_weights[:, :, None], axis=1)
    return mixed.astype(jnp.bfloat16)


def quotient(values, divisor):
    return lax.shift_right_logical(values * ((1 << 16) // divisor + 1), 16)


def iota(shape, axis):
    return lax.broadcasted_iota(jnp.int32, shape, axis)


def column(row):
    size = row.shape[1]
    eye = iota((size, size), 0) == iota((size, size), 1)
    return jnp.sum(jnp.where(eye, row, jnp.zeros((), row.dtype)), axis=1, keepdims=True)


def onehot(mask):
    return jnp.where(mask, 1.0, 0.0).astype(jnp.bfloat16)


def dot(left, right, over=1):
    dims = (((over,), (0,)), ((), ()))
    return lax.dot_general(left, right, dims, preferred_element_type=jnp.float32)


def pick_kernel(slots_dev, key_ref, ids_hbm, plan_hbm, tok_hbm, pick_ref, *refs):
    send_refs, (ids_ref, plan_ref, tok_ref, sems) = refs[:-4], refs[-4:]
    pairs = ((tok_hbm, tok_ref), (ids_hbm, ids_ref), (plan_hbm, plan_ref))
    loads = [pltpu.make_async_copy(a, b, sems.at[i]) for i, (a, b) in enumerate(pairs)]
    for load in loads:
        load.start()
    loads[1].wait()
    loads[2].wait()
    rounds = len(send_refs)
    rows = slots_dev * CAP
    packed = 2 * rows * rounds
    tok_rows, width = tok_ref.shape
    half = width // 2
    slots = plan_ref.shape[1]
    plan = plan_ref[...]
    earlier = (column(plan) == plan) & (iota((slots, slots), 0) < iota((slots, slots), 1))
    repeated = jnp.sum(jnp.where(earlier, 1, 0), axis=0, keepdims=True) > 0
    served = jnp.where(repeated, -1, plan)

    index = iota((packed, 1), 0)
    part = quotient(index, rows)
    entry = quotient(index, CAP)
    rank = index - entry * CAP
    slot = (key_ref[0] ^ lax.shift_right_logical(part, 1)) * slots_dev + entry - part * slots_dev
    side = part & 1
    chosen = jnp.where(iota((packed, slots), 1) == slot, served, 0)
    expert = jnp.sum(chosen, axis=1, keepdims=True)

    ids = jnp.concatenate([ids_ref[...], ids_ref[...]], axis=1)
    lanes = 2 * tok_rows
    lane = iota((packed, lanes), 1)
    same_side = jnp.where(lane < tok_rows, 0, 1) == side
    named = [(expert == ids[k : k + 1, :]) & same_side for k in range(ids.shape[0])]
    either = functools.reduce(jnp.logical_or, named)
    before = onehot(iota((lanes, lanes), 0) < iota((lanes, lanes), 1))
    in_row = dot(onehot(either), before) == rank.astype(jnp.float32)
    for k, mask in enumerate(named):
        pick_ref[k, :, :] = onehot(mask & in_row)
    loads[0].wait()
    stacked = jnp.concatenate([tok_ref[:, :half], tok_ref[:, half:]], axis=0)
    sent = dot(onehot(either & in_row), stacked).astype(jnp.bfloat16)
    for p, send_ref in enumerate(send_refs):
        send_ref[...] = sent[2 * rows * p : 2 * rows * (p + 1), :]


def fetch_kernel(*refs):
    count = (len(refs) - 2) // 2
    sems = refs[-1]
    pieces = sems.shape[1]
    loads = []
    for a in range(count):
        source, target = refs[1 + a], refs[1 + count + a]
        size = source.shape[0] // pieces
        for i in range(pieces):
            piece = pl.ds(i * size, size)
            loads.append(pltpu.make_async_copy(source.at[piece], target.at[piece], sems.at[a, i]))
    for load in loads:
        load.start()
    for load in loads:
        load.wait()


def expert_kernel(slots_dev, bufs, *refs):
    buf_refs = refs[:bufs]
    gate_ref, up_ref, down_hbm, mine_ref, other_ref, x_ref, hidden_ref, down_ref, sems = refs[bufs:]
    ring, blocks, unit, chunk = down_ref.shape
    chunks = down_hbm.shape[2] // chunk
    loads = []
    for i in range(chunks):
        source = down_hbm.at[:, :, pl.ds(i * chunk, chunk)]
        loads.append(pltpu.make_async_copy(source, down_ref.at[i % ring], sems.at[i]))
    for load in loads[:ring]:
        load.start()
    rows = slots_dev * CAP
    total = bufs * rows
    half = buf_refs[0].shape[1]

    got = jnp.concatenate([ref[...] for ref in buf_refs], axis=0)
    place = iota((total, 2 * total), 0)
    place = place + rows * quotient(place, rows)
    lane = iota((total, 2 * total), 1)
    x_ref[:, :half] = dot(onehot(lane == place), got).astype(jnp.bfloat16)
    x_ref[:, half:] = dot(onehot(lane == place + rows), got).astype(jnp.bfloat16)

    index = iota((total, 1), 0)
    row_slot = quotient(index, CAP) - quotient(index, rows) * slots_dev

    def block(b, carry):
        both = dot(x_ref[...], jnp.concatenate([gate_ref[b], up_ref[b]], axis=1))
        gate, upper = both[:, :unit], both[:, unit:]
        value = gate / (1.0 + jnp.exp(-gate)) * upper
        hidden_ref[b] = jnp.where(row_slot == b // HB, value, 0.0).astype(jnp.bfloat16)
        return carry

    lax.fori_loop(0, blocks, block, 0, unroll=UNROLL)
    hidden = jnp.concatenate([hidden_ref[b] for b in range(blocks)], axis=1)
    for i in range(chunks):
        cols = slice(i * chunk, (i + 1) * chunk)
        loads[i].wait()
        part = dot(hidden, down_ref[i % ring].reshape(blocks * unit, chunk))
        mine_ref[:, cols] = part[: total // 2, :]
        other_ref[:, cols] = part[total // 2 :, :].astype(jnp.bfloat16)
        if i + ring < chunks:
            loads[i + ring].start()


def sum_kernel(rows, mine_ref, got_ref, *send_refs):
    total = mine_ref.shape[0]
    half = mine_ref.shape[1] // 2
    summed = (mine_ref[...] + got_ref[...].astype(jnp.float32)).astype(jnp.bfloat16)
    stacked = jnp.concatenate([summed[:, :half], summed[:, half:]], axis=0)
    index = iota((2 * total, 2 * total), 0)
    part = quotient(index, rows)
    source = index - rows * part + rows * lax.shift_right_logical(part, 1) + total * (part & 1)
    packed = dot(onehot(iota((2 * total, 2 * total), 1) == source), stacked).astype(jnp.bfloat16)
    for p, send_ref in enumerate(send_refs):
        send_ref[...] = packed[2 * rows * p : 2 * rows * (p + 1), :]


def combine_kernel(bufs, core_ref, pick_ref, weight_ref, *refs):
    got = jnp.concatenate([ref[...] for ref in refs[:bufs]], axis=0)
    keep_ref, give_ref, sum_ref = refs[bufs:]
    tok_rows = keep_ref.shape[0]
    mixed = None
    for k in range(pick_ref.shape[0]):
        weight = column(weight_ref[k : k + 1, :])
        term = dot(pick_ref[k], got, 0) * jnp.concatenate([weight, weight], axis=0)
        mixed = term if mixed is None else mixed + term
    sum_ref[...] = mixed
    core = core_ref[0]
    keep_ref[...] = sum_ref[pl.ds(pl.multiple_of(core * tok_rows, 8), tok_rows), :]
    give_ref[...] = sum_ref[pl.ds(pl.multiple_of((1 - core) * tok_rows, 8), tok_rows), :].astype(jnp.bfloat16)


ANY = pl.BlockSpec(memory_space=pl.ANY)
HBM = pl.BlockSpec(memory_space=pltpu.HBM)
VMEM = pl.BlockSpec(memory_space=pltpu.VMEM)
SMEM = pl.BlockSpec(memory_space=pltpu.SMEM)


def from_hbm(array):
    return pltpu.with_memory_space_constraint(array, pltpu.HBM)


def params(mib):
    return pltpu.CompilerParams(vmem_limit_bytes=mib * MIB)


def shards_paired(tokens, expert_ids, route_weights, slot_plan, w_gate, w_up, w_down):
    chips = lax.axis_size("expert")
    rounds = chips // 2
    core = lax.axis_index("tensor").astype(jnp.int32)
    chip = lax.axis_index("expert").astype(jnp.int32)
    slots_dev = w_gate.shape[0] // HB
    rows = slots_dev * CAP
    tok_rows, width = tokens.shape
    half = width // 2
    picks = expert_ids.shape[1]
    packed = jax.ShapeDtypeStruct((2 * rows, half), jnp.bfloat16)
    key = (chip ^ (core * rounds)).reshape(1)

    def travel(arrays):
        return [
            lax.ppermute(
                array,
                ("expert", "tensor"),
                [(2 * i + c, 2 * (i ^ (p + rounds * c)) + c) for i in range(chips) for c in range(2)],
            )
            for p, array in enumerate(arrays)
        ]

    pick, *sent = pl.pallas_call(
        functools.partial(pick_kernel, slots_dev),
        out_shape=[jax.ShapeDtypeStruct((picks, 2 * rows * rounds, 2 * tok_rows), jnp.bfloat16)] + [packed] * rounds,
        in_specs=[SMEM, HBM, HBM, HBM],
        out_specs=[VMEM] * (1 + rounds),
        scratch_shapes=[
            pltpu.VMEM((picks, tok_rows), jnp.int32),
            pltpu.VMEM((1, slot_plan.shape[0]), jnp.int32),
            pltpu.VMEM((tok_rows, width), jnp.bfloat16),
            pltpu.SemaphoreType.DMA((3,)),
        ],
        compiler_params=params(16),
        name="pick_rows",
    )(key, *[from_hbm(a) for a in (expert_ids.T, slot_plan.reshape(1, -1), tokens)])

    weights = [w_gate, w_up]
    held = pl.pallas_call(
            fetch_kernel,
            out_shape=[pltpu.VMEM(w.shape, w.dtype) for w in weights[:2]],
            in_specs=[ANY] + [HBM] * 2,
            out_specs=[ANY] * 2,
            scratch_shapes=[pltpu.SemaphoreType.DMA((2, 4))],
            compiler_params=params(1),
            cost_estimate=pl.CostEstimate(flops=0, bytes_accessed=2 * 2 * w_gate.size, transcendentals=0),
            name="fetch",
        )(sent[-1], *[from_hbm(w) for w in weights])

    got, held = lax.optimization_barrier((travel(sent), held))
    got = got + [swapped(array, "tensor", 0) for array in got]

    total = chips * rows
    blocks, _, unit = w_gate.shape
    mine, other = pl.pallas_call(
        functools.partial(expert_kernel, slots_dev, chips),
        out_shape=[
            jax.ShapeDtypeStruct((total // 2, width), jnp.float32),
            jax.ShapeDtypeStruct((total // 2, width), jnp.bfloat16),
        ],
        in_specs=[VMEM] * (chips + 2) + [HBM],
        out_specs=[VMEM] * 2,
        scratch_shapes=[
            pltpu.VMEM((total, width), jnp.bfloat16),
            pltpu.VMEM((blocks, total, unit), jnp.bfloat16),
            pltpu.VMEM((RING, blocks, unit, COLUMNS), jnp.bfloat16),
            pltpu.SemaphoreType.DMA((width // COLUMNS,)),
        ],
        compiler_params=params(LIMIT),
        name="experts",
    )(*got, *held, from_hbm(w_down))

    back = pl.pallas_call(
        functools.partial(sum_kernel, rows),
        out_shape=[packed] * rounds,
        in_specs=[VMEM, VMEM],
        out_specs=[VMEM] * rounds,
        compiler_params=params(16),
        name="sum_cores",
    )(mine, swapped(other, "tensor", 0))

    home = travel(back)
    keep, give = pl.pallas_call(
        functools.partial(combine_kernel, rounds),
        out_shape=[
            jax.ShapeDtypeStruct((tok_rows, half), jnp.float32),
            jax.ShapeDtypeStruct((tok_rows, half), jnp.bfloat16),
        ],
        in_specs=[SMEM] + [VMEM] * (2 + rounds),
        out_specs=[VMEM] * 2,
        scratch_shapes=[pltpu.VMEM((2 * tok_rows, half), jnp.float32)],
        compiler_params=params(16),
        name="combine",
    )(core.reshape(1), pick, route_weights.T, *home)
    return (keep + swapped(give, "tensor", 0).astype(jnp.float32)).astype(jnp.bfloat16)


def solution(mesh):
    in_specs = (
        P(("groups", "expert"), None),
        P(("groups", "expert"), None),
        P(("groups", "expert"), None),
        P("groups"),
        P(("groups", "expert"), None, "tensor"),
        P(("groups", "expert"), None, "tensor"),
        P(("groups", "expert"), "tensor", None),
    )
    out_specs = P(("groups", "expert"), "tensor")
    chips = mesh.shape["expert"]
    paired = mesh.shape["tensor"] == 2 and chips in (2, 4, 8) and SLOTS % chips == 0
    body = shards_paired if paired else shards
    return jax.shard_map(body, mesh=mesh, in_specs=in_specs, out_specs=out_specs, check_vma=False)
```

```python
import functools
import jax
import jax.numpy as jnp
import numpy as np
from jax import lax
from jax.experimental import pallas as pl
from jax.experimental.pallas import tpu as pltpu
from jax.sharding import PartitionSpec as P

HB = 4
SLOTS = 32
EXPERTS = 28
CAP = 5
UNROLL = 8
COLUMNS = 896
LIMIT = 15
RING = 3
MIB = 1 << 20


def swapped(shard, axis, stride):
    return lax.ppermute(shard, axis, [(i, i ^ 1 << stride) for i in range(lax.axis_size(axis))])


def shards(tokens, expert_ids, route_weights, slot_plan, w_gate, w_up, w_down):
    devices = lax.axis_size("expert")
    core = lax.axis_index("tensor")
    blocks_dev = w_gate.shape[0]
    slots_dev = max(1, blocks_dev // HB)
    width = tokens.shape[1]
    half = width // 2
    tok_rows = tokens.shape[0]
    picks_tok = expert_ids.shape[1]
    flat_ids = expert_ids.reshape(-1)
    slot_iota = jnp.arange(SLOTS, dtype=jnp.int32)
    expert_iota = jnp.arange(EXPERTS, dtype=jnp.int32)
    hosted = slot_plan[None, :] == expert_iota[:, None]
    first_slot = jnp.min(jnp.where(hosted, slot_iota[None, :], SLOTS), axis=1)
    naming = (flat_ids[:, None] == expert_iota[None, :]).astype(jnp.int32)
    lowest = jnp.sum(naming * first_slot[None, :], axis=1)
    placed = (lowest[:, None] == slot_iota[None, :]).astype(jnp.int32)
    position = jnp.sum((jnp.cumsum(placed, axis=0) - placed) * placed, axis=1)
    entry_iota = np.arange(devices * slots_dev)
    dest_slot = jnp.asarray(
        entry_iota // slots_dev * blocks_dev // HB + entry_iota % slots_dev, jnp.int32
    )
    slot_match = dest_slot[:, None] == lowest[None, :]
    row_match = jnp.arange(CAP, dtype=jnp.int32)[:, None] == position[None, :]
    routing = (slot_match[:, None, :] & row_match[None, :, :]).astype(jnp.int32)
    routing = routing.reshape(devices * slots_dev * CAP, tok_rows, picks_tok)
    tok_iota = jnp.arange(tok_rows, dtype=jnp.int32)
    source_row = jnp.sum(routing * tok_iota[None, :, None], axis=(1, 2))
    live_row = jnp.sum(routing, axis=(1, 2)) > 0
    block_slot = np.arange(blocks_dev) // HB
    outgoing = jnp.where(live_row[:, None], tokens[source_row], jnp.zeros((), jnp.bfloat16))
    outgoing = outgoing.reshape(devices, slots_dev, CAP, width)
    picked = jnp.take(
        lax.all_to_all(outgoing, "expert", split_axis=0, concat_axis=0, tiled=True),
        block_slot,
        axis=1,
    )
    gate = jnp.einsum("nbcd,bdu->nbcu", picked, w_gate, preferred_element_type=jnp.float32)
    upper = jnp.einsum("nbcd,bdu->nbcu", picked, w_up, preferred_element_type=jnp.float32)
    hidden = (jax.nn.silu(gate) * upper).astype(jnp.bfloat16)
    result = jnp.einsum("nbcu,bud->nbcd", hidden, w_down, preferred_element_type=jnp.float32)
    result = lax.optimization_barrier(result.astype(jnp.bfloat16))
    mine = lax.dynamic_slice_in_dim(result, core * half, half, 3)
    other = lax.dynamic_slice_in_dim(result, (1 - core) * half, half, 3)
    partner = swapped(other, "tensor", 0)
    outputs = (mine.astype(jnp.float32) + partner.astype(jnp.float32)).astype(jnp.bfloat16)
    returned = lax.all_to_all(outputs, "expert", split_axis=0, concat_axis=0, tiled=True)
    returned = returned.reshape(-1, half)
    block_iota = jnp.arange(HB, dtype=jnp.int32)
    row_index = (lowest[:, None] * HB + block_iota[None, :]) * CAP + position[:, None]
    gathered = returned[row_index.reshape(-1)].reshape(tok_rows, picks_tok, HB, half)
    summed = jnp.sum(gathered.astype(jnp.float32), axis=2)
    mixed = jnp.sum(summed * route_weights[:, :, None], axis=1)
    return mixed.astype(jnp.bfloat16)


def quotient(values, divisor):
    return lax.shift_right_logical(values * ((1 << 16) // divisor + 1), 16)


def iota(shape, axis):
    return lax.broadcasted_iota(jnp.int32, shape, axis)


def column(row):
    size = row.shape[1]
    eye = iota((size, size), 0) == iota((size, size), 1)
    return jnp.sum(jnp.where(eye, row, jnp.zeros((), row.dtype)), axis=1, keepdims=True)


def onehot(mask):
    return jnp.where(mask, 1.0, 0.0).astype(jnp.bfloat16)


def dot(left, right, over=1):
    dims = (((over,), (0,)), ((), ()))
    return lax.dot_general(left, right, dims, preferred_element_type=jnp.float32)


def turns(rounds):
    return sorted(range(rounds), key=lambda p: (p < 2, p if p > 1 else -p))


def pick_kernel(slots_dev, key_ref, ids_hbm, plan_hbm, tok_hbm, pick_ref, *refs):
    send_refs, (ids_ref, plan_ref, tok_ref, sems) = refs[:-4], refs[-4:]
    pairs = ((tok_hbm, tok_ref), (ids_hbm, ids_ref), (plan_hbm, plan_ref))
    loads = [pltpu.make_async_copy(a, b, sems.at[i]) for i, (a, b) in enumerate(pairs)]
    for load in loads:
        load.start()
    loads[1].wait()
    loads[2].wait()
    rounds = len(send_refs)
    rows = slots_dev * CAP
    packed = 2 * rows * rounds
    tok_rows, width = tok_ref.shape
    half = width // 2
    slots = plan_ref.shape[1]
    plan = plan_ref[...]
    earlier = (column(plan) == plan) & (iota((slots, slots), 0) < iota((slots, slots), 1))
    repeated = jnp.sum(jnp.where(earlier, 1, 0), axis=0, keepdims=True) > 0
    served = jnp.where(repeated, -1, plan)

    index = iota((packed, 1), 0)
    part = quotient(index, rows)
    entry = quotient(index, CAP)
    rank = index - entry * CAP
    turn = lax.shift_right_logical(part, 1)
    distance = sum(jnp.where(turn == q, p, 0) for q, p in enumerate(turns(rounds)))
    slot = (key_ref[0] ^ distance) * slots_dev + entry - part * slots_dev
    side = part & 1
    chosen = jnp.where(iota((packed, slots), 1) == slot, served, 0)
    expert = jnp.sum(chosen, axis=1, keepdims=True)

    ids = jnp.concatenate([ids_ref[...], ids_ref[...]], axis=1)
    lanes = 2 * tok_rows
    lane = iota((packed, lanes), 1)
    same_side = jnp.where(lane < tok_rows, 0, 1) == side
    named = [(expert == ids[k : k + 1, :]) & same_side for k in range(ids.shape[0])]
    either = functools.reduce(jnp.logical_or, named)
    before = onehot(iota((lanes, lanes), 0) < iota((lanes, lanes), 1))
    in_row = dot(onehot(either), before) == rank.astype(jnp.float32)
    for k, mask in enumerate(named):
        pick_ref[k, :, :] = onehot(mask & in_row)
    loads[0].wait()
    stacked = jnp.concatenate([tok_ref[:, :half], tok_ref[:, half:]], axis=0)
    sent = dot(onehot(either & in_row), stacked).astype(jnp.bfloat16)
    for p, send_ref in enumerate(send_refs):
        send_ref[...] = sent[2 * rows * p : 2 * rows * (p + 1), :]


def fetch_kernel(*refs):
    count = (len(refs) - 2) // 2
    sems = refs[-1]
    pieces = sems.shape[1]
    loads = []
    for a in range(count):
        source, target = refs[1 + a], refs[1 + count + a]
        size = source.shape[0] // pieces
        for i in range(pieces):
            piece = pl.ds(i * size, size)
            loads.append(pltpu.make_async_copy(source.at[piece], target.at[piece], sems.at[a, i]))
    for load in loads:
        load.start()
    for load in loads:
        load.wait()


def expert_kernel(slots_dev, bufs, *refs):
    buf_refs = refs[:bufs]
    gate_ref, up_ref, down_hbm, mine_ref, other_ref, x_ref, hidden_ref, down_ref, sems = refs[bufs:]
    ring, blocks, unit, chunk = down_ref.shape
    chunks = down_hbm.shape[2] // chunk
    loads = []
    for i in range(chunks):
        source = down_hbm.at[:, :, pl.ds(i * chunk, chunk)]
        loads.append(pltpu.make_async_copy(source, down_ref.at[i % ring], sems.at[i]))
    for load in loads[:ring]:
        load.start()
    rows = slots_dev * CAP
    total = bufs * rows
    half = buf_refs[0].shape[1]

    got = jnp.concatenate([ref[...] for ref in buf_refs], axis=0)
    place = iota((total, 2 * total), 0)
    place = place + rows * quotient(place, rows)
    lane = iota((total, 2 * total), 1)
    x_ref[:, :half] = dot(onehot(lane == place), got).astype(jnp.bfloat16)
    x_ref[:, half:] = dot(onehot(lane == place + rows), got).astype(jnp.bfloat16)

    index = iota((total, 1), 0)
    row_slot = quotient(index, CAP) - quotient(index, rows) * slots_dev

    def block(b, carry):
        both = dot(x_ref[...], jnp.concatenate([gate_ref[b], up_ref[b]], axis=1))
        gate, upper = both[:, :unit], both[:, unit:]
        value = gate / (1.0 + jnp.exp(-gate)) * upper
        hidden_ref[b] = jnp.where(row_slot == b // HB, value, 0.0).astype(jnp.bfloat16)
        return carry

    lax.fori_loop(0, blocks, block, 0, unroll=UNROLL)
    hidden = jnp.concatenate([hidden_ref[b] for b in range(blocks)], axis=1)
    for i in range(chunks):
        cols = slice(i * chunk, (i + 1) * chunk)
        loads[i].wait()
        part = dot(hidden, down_ref[i % ring].reshape(blocks * unit, chunk))
        mine_ref[:, cols] = part[: total // 2, :]
        other_ref[:, cols] = part[total // 2 :, :].astype(jnp.bfloat16)
        if i + ring < chunks:
            loads[i + ring].start()


def sum_kernel(rows, mine_ref, got_ref, *send_refs):
    total = mine_ref.shape[0]
    half = mine_ref.shape[1] // 2
    summed = (mine_ref[...] + got_ref[...].astype(jnp.float32)).astype(jnp.bfloat16)
    stacked = jnp.concatenate([summed[:, :half], summed[:, half:]], axis=0)
    index = iota((2 * total, 2 * total), 0)
    part = quotient(index, rows)
    source = index - rows * part + rows * lax.shift_right_logical(part, 1) + total * (part & 1)
    packed = dot(onehot(iota((2 * total, 2 * total), 1) == source), stacked).astype(jnp.bfloat16)
    for p, send_ref in enumerate(send_refs):
        send_ref[...] = packed[2 * rows * p : 2 * rows * (p + 1), :]


def combine_kernel(bufs, core_ref, pick_ref, weight_ref, *refs):
    got = jnp.concatenate([ref[...] for ref in refs[:bufs]], axis=0)
    keep_ref, give_ref, sum_ref = refs[bufs:]
    tok_rows = keep_ref.shape[0]
    mixed = None
    for k in range(pick_ref.shape[0]):
        weight = column(weight_ref[k : k + 1, :])
        term = dot(pick_ref[k], got, 0) * jnp.concatenate([weight, weight], axis=0)
        mixed = term if mixed is None else mixed + term
    sum_ref[...] = mixed
    core = core_ref[0]
    keep_ref[...] = sum_ref[pl.ds(pl.multiple_of(core * tok_rows, 8), tok_rows), :]
    give_ref[...] = sum_ref[pl.ds(pl.multiple_of((1 - core) * tok_rows, 8), tok_rows), :].astype(jnp.bfloat16)


ANY = pl.BlockSpec(memory_space=pl.ANY)
HBM = pl.BlockSpec(memory_space=pltpu.HBM)
VMEM = pl.BlockSpec(memory_space=pltpu.VMEM)
SMEM = pl.BlockSpec(memory_space=pltpu.SMEM)


def from_hbm(array):
    return pltpu.with_memory_space_constraint(array, pltpu.HBM)


def params(mib):
    return pltpu.CompilerParams(vmem_limit_bytes=mib * MIB)


def shards_paired(tokens, expert_ids, route_weights, slot_plan, w_gate, w_up, w_down):
    chips = lax.axis_size("expert")
    rounds = chips // 2
    core = lax.axis_index("tensor").astype(jnp.int32)
    chip = lax.axis_index("expert").astype(jnp.int32)
    slots_dev = w_gate.shape[0] // HB
    rows = slots_dev * CAP
    tok_rows, width = tokens.shape
    half = width // 2
    picks = expert_ids.shape[1]
    packed = jax.ShapeDtypeStruct((2 * rows, half), jnp.bfloat16)
    key = (chip ^ (core * rounds)).reshape(1)

    def travel(arrays):
        return [
            lax.ppermute(
                array,
                ("expert", "tensor"),
                [(2 * i + c, 2 * (i ^ (p + rounds * c)) + c) for i in range(chips) for c in range(2)],
            )
            for p, array in zip(turns(rounds), arrays)
        ]

    pick, *sent = pl.pallas_call(
        functools.partial(pick_kernel, slots_dev),
        out_shape=[jax.ShapeDtypeStruct((picks, 2 * rows * rounds, 2 * tok_rows), jnp.bfloat16)] + [packed] * rounds,
        in_specs=[SMEM, HBM, HBM, HBM],
        out_specs=[VMEM] * (1 + rounds),
        scratch_shapes=[
            pltpu.VMEM((picks, tok_rows), jnp.int32),
            pltpu.VMEM((1, slot_plan.shape[0]), jnp.int32),
            pltpu.VMEM((tok_rows, width), jnp.bfloat16),
            pltpu.SemaphoreType.DMA((3,)),
        ],
        compiler_params=params(16),
        name="pick_rows",
    )(key, *[from_hbm(a) for a in (expert_ids.T, slot_plan.reshape(1, -1), tokens)])

    weights = [w_gate, w_up]
    held = pl.pallas_call(
            fetch_kernel,
            out_shape=[pltpu.VMEM(w.shape, w.dtype) for w in weights[:2]],
            in_specs=[ANY] + [HBM] * 2,
            out_specs=[ANY] * 2,
            scratch_shapes=[pltpu.SemaphoreType.DMA((2, 4))],
            compiler_params=params(1),
            cost_estimate=pl.CostEstimate(flops=0, bytes_accessed=2 * 2 * w_gate.size, transcendentals=0),
            name="fetch",
        )(sent[-1], *[from_hbm(w) for w in weights])

    got, held = lax.optimization_barrier((travel(sent), held))
    got = got + [swapped(array, "tensor", 0) for array in got]

    total = chips * rows
    blocks, _, unit = w_gate.shape
    mine, other = pl.pallas_call(
        functools.partial(expert_kernel, slots_dev, chips),
        out_shape=[
            jax.ShapeDtypeStruct((total // 2, width), jnp.float32),
            jax.ShapeDtypeStruct((total // 2, width), jnp.bfloat16),
        ],
        in_specs=[VMEM] * (chips + 2) + [HBM],
        out_specs=[VMEM] * 2,
        scratch_shapes=[
            pltpu.VMEM((total, width), jnp.bfloat16),
            pltpu.VMEM((blocks, total, unit), jnp.bfloat16),
            pltpu.VMEM((RING, blocks, unit, COLUMNS), jnp.bfloat16),
            pltpu.SemaphoreType.DMA((width // COLUMNS,)),
        ],
        compiler_params=params(LIMIT),
        name="experts",
    )(*got, *held, from_hbm(w_down))

    back = pl.pallas_call(
        functools.partial(sum_kernel, rows),
        out_shape=[packed] * rounds,
        in_specs=[VMEM, VMEM],
        out_specs=[VMEM] * rounds,
        compiler_params=params(16),
        name="sum_cores",
    )(mine, swapped(other, "tensor", 0))

    home = travel(back)
    keep, give = pl.pallas_call(
        functools.partial(combine_kernel, rounds),
        out_shape=[
            jax.ShapeDtypeStruct((tok_rows, half), jnp.float32),
            jax.ShapeDtypeStruct((tok_rows, half), jnp.bfloat16),
        ],
        in_specs=[SMEM] + [VMEM] * (2 + rounds),
        out_specs=[VMEM] * 2,
        scratch_shapes=[pltpu.VMEM((2 * tok_rows, half), jnp.float32)],
        compiler_params=params(16),
        name="combine",
    )(core.reshape(1), pick, route_weights.T, *home)
    return (keep + swapped(give, "tensor", 0).astype(jnp.float32)).astype(jnp.bfloat16)


def solution(mesh):
    in_specs = (
        P(("groups", "expert"), None),
        P(("groups", "expert"), None),
        P(("groups", "expert"), None),
        P("groups"),
        P(("groups", "expert"), None, "tensor"),
        P(("groups", "expert"), None, "tensor"),
        P(("groups", "expert"), "tensor", None),
    )
    out_specs = P(("groups", "expert"), "tensor")
    chips = mesh.shape["expert"]
    paired = mesh.shape["tensor"] == 2 and chips in (2, 4, 8) and SLOTS % chips == 0
    body = shards_paired if paired else shards
    return jax.shard_map(body, mesh=mesh, in_specs=in_specs, out_specs=out_specs, check_vma=False)
```

```python
import functools
import jax
import jax.numpy as jnp
import numpy as np
from jax import lax
from jax.experimental import pallas as pl
from jax.experimental.pallas import tpu as pltpu
from jax.sharding import PartitionSpec as P

HB = 4
SLOTS = 32
EXPERTS = 28
CAP = 5
UNROLL = 4
COLUMNS = 896
LIMIT = 26
RING = 3
PIECE = 2
EARLY = 4
MIB = 1 << 20


def swapped(shard, axis, stride):
    return lax.ppermute(shard, axis, [(i, i ^ 1 << stride) for i in range(lax.axis_size(axis))])


def shards(tokens, expert_ids, route_weights, slot_plan, w_gate, w_up, w_down):
    devices = lax.axis_size("expert")
    core = lax.axis_index("tensor")
    blocks_dev = w_gate.shape[0]
    slots_dev = max(1, blocks_dev // HB)
    width = tokens.shape[1]
    half = width // 2
    tok_rows = tokens.shape[0]
    picks_tok = expert_ids.shape[1]
    flat_ids = expert_ids.reshape(-1)
    slot_iota = jnp.arange(SLOTS, dtype=jnp.int32)
    expert_iota = jnp.arange(EXPERTS, dtype=jnp.int32)
    hosted = slot_plan[None, :] == expert_iota[:, None]
    first_slot = jnp.min(jnp.where(hosted, slot_iota[None, :], SLOTS), axis=1)
    naming = (flat_ids[:, None] == expert_iota[None, :]).astype(jnp.int32)
    lowest = jnp.sum(naming * first_slot[None, :], axis=1)
    placed = (lowest[:, None] == slot_iota[None, :]).astype(jnp.int32)
    position = jnp.sum((jnp.cumsum(placed, axis=0) - placed) * placed, axis=1)
    entry_iota = np.arange(devices * slots_dev)
    dest_slot = jnp.asarray(
        entry_iota // slots_dev * blocks_dev // HB + entry_iota % slots_dev, jnp.int32
    )
    slot_match = dest_slot[:, None] == lowest[None, :]
    row_match = jnp.arange(CAP, dtype=jnp.int32)[:, None] == position[None, :]
    routing = (slot_match[:, None, :] & row_match[None, :, :]).astype(jnp.int32)
    routing = routing.reshape(devices * slots_dev * CAP, tok_rows, picks_tok)
    tok_iota = jnp.arange(tok_rows, dtype=jnp.int32)
    source_row = jnp.sum(routing * tok_iota[None, :, None], axis=(1, 2))
    live_row = jnp.sum(routing, axis=(1, 2)) > 0
    block_slot = np.arange(blocks_dev) // HB
    outgoing = jnp.where(live_row[:, None], tokens[source_row], jnp.zeros((), jnp.bfloat16))
    outgoing = outgoing.reshape(devices, slots_dev, CAP, width)
    picked = jnp.take(
        lax.all_to_all(outgoing, "expert", split_axis=0, concat_axis=0, tiled=True),
        block_slot,
        axis=1,
    )
    gate = jnp.einsum("nbcd,bdu->nbcu", picked, w_gate, preferred_element_type=jnp.float32)
    upper = jnp.einsum("nbcd,bdu->nbcu", picked, w_up, preferred_element_type=jnp.float32)
    hidden = (jax.nn.silu(gate) * upper).astype(jnp.bfloat16)
    result = jnp.einsum("nbcu,bud->nbcd", hidden, w_down, preferred_element_type=jnp.float32)
    result = lax.optimization_barrier(result.astype(jnp.bfloat16))
    mine = lax.dynamic_slice_in_dim(result, core * half, half, 3)
    other = lax.dynamic_slice_in_dim(result, (1 - core) * half, half, 3)
    partner = swapped(other, "tensor", 0)
    outputs = (mine.astype(jnp.float32) + partner.astype(jnp.float32)).astype(jnp.bfloat16)
    returned = lax.all_to_all(outputs, "expert", split_axis=0, concat_axis=0, tiled=True)
    returned = returned.reshape(-1, half)
    block_iota = jnp.arange(HB, dtype=jnp.int32)
    row_index = (lowest[:, None] * HB + block_iota[None, :]) * CAP + position[:, None]
    gathered = returned[row_index.reshape(-1)].reshape(tok_rows, picks_tok, HB, half)
    summed = jnp.sum(gathered.astype(jnp.float32), axis=2)
    mixed = jnp.sum(summed * route_weights[:, :, None], axis=1)
    return mixed.astype(jnp.bfloat16)


def quotient(values, divisor):
    return lax.shift_right_logical(values * ((1 << 16) // divisor + 1), 16)


def iota(shape, axis):
    return lax.broadcasted_iota(jnp.int32, shape, axis)


def column(row):
    size = row.shape[1]
    eye = iota((size, size), 0) == iota((size, size), 1)
    return jnp.sum(jnp.where(eye, row, jnp.zeros((), row.dtype)), axis=1, keepdims=True)


def onehot(mask):
    return jnp.where(mask, 1.0, 0.0).astype(jnp.bfloat16)


def dot(left, right, over=1):
    dims = (((over,), (0,)), ((), ()))
    return lax.dot_general(left, right, dims, preferred_element_type=jnp.float32)


def turns(rounds):
    return sorted(range(rounds), key=lambda p: (p < 2, p if p > 1 else -p))


def pick_kernel(slots_dev, key_ref, ids_hbm, plan_hbm, tok_hbm, pick_ref, *refs):
    send_refs, (ids_ref, plan_ref, tok_ref, sems) = refs[:-4], refs[-4:]
    pairs = ((tok_hbm, tok_ref), (ids_hbm, ids_ref), (plan_hbm, plan_ref))
    loads = [pltpu.make_async_copy(a, b, sems.at[i]) for i, (a, b) in enumerate(pairs)]
    for load in loads:
        load.start()
    loads[1].wait()
    loads[2].wait()
    rounds = len(send_refs)
    rows = slots_dev * CAP
    packed = 2 * rows * rounds
    tok_rows, width = tok_ref.shape
    half = width // 2
    slots = plan_ref.shape[1]
    plan = plan_ref[...]
    earlier = (column(plan) == plan) & (iota((slots, slots), 0) < iota((slots, slots), 1))
    repeated = jnp.sum(jnp.where(earlier, 1, 0), axis=0, keepdims=True) > 0
    served = jnp.where(repeated, -1, plan)

    index = iota((packed, 1), 0)
    part = quotient(index, rows)
    entry = quotient(index, CAP)
    rank = index - entry * CAP
    turn = lax.shift_right_logical(part, 1)
    distance = sum(jnp.where(turn == q, p, 0) for q, p in enumerate(turns(rounds)))
    slot = (key_ref[0] ^ distance) * slots_dev + entry - part * slots_dev
    side = part & 1
    chosen = jnp.where(iota((packed, slots), 1) == slot, served, 0)
    expert = jnp.sum(chosen, axis=1, keepdims=True)

    ids = jnp.concatenate([ids_ref[...], ids_ref[...]], axis=1)
    lanes = 2 * tok_rows
    lane = iota((packed, lanes), 1)
    same_side = jnp.where(lane < tok_rows, 0, 1) == side
    named = [(expert == ids[k : k + 1, :]) & same_side for k in range(ids.shape[0])]
    either = functools.reduce(jnp.logical_or, named)
    before = onehot(iota((lanes, lanes), 0) < iota((lanes, lanes), 1))
    in_row = dot(onehot(either), before) == rank.astype(jnp.float32)
    for k, mask in enumerate(named):
        pick_ref[k, :, :] = onehot(mask & in_row)
    loads[0].wait()
    stacked = jnp.concatenate([tok_ref[:, :half], tok_ref[:, half:]], axis=0)
    sent = dot(onehot(either & in_row), stacked).astype(jnp.bfloat16)
    for p, send_ref in enumerate(send_refs):
        send_ref[...] = sent[2 * rows * p : 2 * rows * (p + 1), :]


def fetch_kernel(*refs):
    count = (len(refs) - 2) // 2
    sems = refs[-1]
    pieces = sems.shape[1]
    loads = []
    for a in range(count):
        source, target = refs[1 + a], refs[1 + count + a]
        size = target.shape[0] // pieces
        for i in range(pieces):
            piece = pl.ds(i * size, size)
            loads.append(pltpu.make_async_copy(source.at[piece], target.at[piece], sems.at[a, i]))
    for load in loads:
        load.start()
    for load in loads:
        load.wait()


def expert_kernel(slots_dev, bufs, *refs):
    buf_refs = refs[:bufs]
    gate_ref, up_ref, up_hbm, down_hbm, mine_ref, other_ref = refs[bufs : bufs + 6]
    x_ref, hidden_ref, late_ref, down_ref, late_sems, sems = refs[bufs + 6 :]
    held = up_ref.shape[0]
    ring, blocks, unit, chunk = down_ref.shape
    chunks = down_hbm.shape[2] // chunk
    loads = []
    for i in range(chunks):
        source = down_hbm.at[:, :, pl.ds(i * chunk, chunk)]
        loads.append(pltpu.make_async_copy(source, down_ref.at[i % ring], sems.at[i]))

    def late(i):
        part = pl.ds(i * PIECE, PIECE)
        source = up_hbm.at[pl.ds(held + i * PIECE, PIECE)]
        return pltpu.make_async_copy(source, late_ref.at[part], late_sems.at[i])

    for i in range((blocks - held) // PIECE):
        late(i).start()
    for load in loads[:ring]:
        load.start()
    rows = slots_dev * CAP
    total = bufs * rows
    half = buf_refs[0].shape[1]

    got = jnp.concatenate([ref[...] for ref in buf_refs], axis=0)
    place = iota((total, 2 * total), 0)
    place = place + rows * quotient(place, rows)
    lane = iota((total, 2 * total), 1)
    x_ref[:, :half] = dot(onehot(lane == place), got).astype(jnp.bfloat16)
    x_ref[:, half:] = dot(onehot(lane == place + rows), got).astype(jnp.bfloat16)

    index = iota((total, 1), 0)
    row_slot = quotient(index, CAP) - quotient(index, rows) * slots_dev

    def block(b, up):
        both = dot(x_ref[...], jnp.concatenate([gate_ref[b], up], axis=1))
        gate, upper = both[:, :unit], both[:, unit:]
        value = gate / (1.0 + jnp.exp(-gate)) * upper
        hidden_ref[b] = jnp.where(row_slot == b // HB, value, 0.0).astype(jnp.bfloat16)

    def early_block(b, carry):
        block(b, up_ref[b])
        return carry

    def late_piece(i, carry):
        late(i).wait()
        for j in range(PIECE):
            block(held + i * PIECE + j, late_ref[i * PIECE + j])
        return carry

    lax.fori_loop(0, held, early_block, 0, unroll=min(held, UNROLL))
    lax.fori_loop(0, (blocks - held) // PIECE, late_piece, 0, unroll=min((blocks - held), UNROLL) // PIECE)
    hidden = jnp.concatenate([hidden_ref[b] for b in range(blocks)], axis=1)
    for i in range(chunks):
        cols = slice(i * chunk, (i + 1) * chunk)
        loads[i].wait()
        part = dot(hidden, down_ref[i % ring].reshape(blocks * unit, chunk))
        mine_ref[:, cols] = part[: total // 2, :]
        other_ref[:, cols] = part[total // 2 :, :].astype(jnp.bfloat16)
        if i + ring < chunks:
            loads[i + ring].start()


def sum_kernel(rows, mine_ref, got_ref, *send_refs):
    total = mine_ref.shape[0]
    half = mine_ref.shape[1] // 2
    summed = (mine_ref[...] + got_ref[...].astype(jnp.float32)).astype(jnp.bfloat16)
    stacked = jnp.concatenate([summed[:, :half], summed[:, half:]], axis=0)
    index = iota((2 * total, 2 * total), 0)
    part = quotient(index, rows)
    source = index - rows * part + rows * lax.shift_right_logical(part, 1) + total * (part & 1)
    packed = dot(onehot(iota((2 * total, 2 * total), 1) == source), stacked).astype(jnp.bfloat16)
    for p, send_ref in enumerate(send_refs):
        send_ref[...] = packed[2 * rows * p : 2 * rows * (p + 1), :]


def combine_kernel(bufs, core_ref, pick_ref, weight_ref, *refs):
    got = jnp.concatenate([ref[...] for ref in refs[:bufs]], axis=0)
    keep_ref, give_ref, sum_ref = refs[bufs:]
    tok_rows = keep_ref.shape[0]
    mixed = None
    for k in range(pick_ref.shape[0]):
        weight = column(weight_ref[k : k + 1, :])
        term = dot(pick_ref[k], got, 0) * jnp.concatenate([weight, weight], axis=0)
        mixed = term if mixed is None else mixed + term
    sum_ref[...] = mixed
    core = core_ref[0]
    keep_ref[...] = sum_ref[pl.ds(pl.multiple_of(core * tok_rows, 8), tok_rows), :]
    give_ref[...] = sum_ref[pl.ds(pl.multiple_of((1 - core) * tok_rows, 8), tok_rows), :].astype(jnp.bfloat16)


ANY = pl.BlockSpec(memory_space=pl.ANY)
HBM = pl.BlockSpec(memory_space=pltpu.HBM)
VMEM = pl.BlockSpec(memory_space=pltpu.VMEM)
SMEM = pl.BlockSpec(memory_space=pltpu.SMEM)


def from_hbm(array):
    return pltpu.with_memory_space_constraint(array, pltpu.HBM)


def params(mib):
    return pltpu.CompilerParams(vmem_limit_bytes=mib * MIB)


def shards_paired(tokens, expert_ids, route_weights, slot_plan, w_gate, w_up, w_down):
    chips = lax.axis_size("expert")
    rounds = chips // 2
    core = lax.axis_index("tensor").astype(jnp.int32)
    chip = lax.axis_index("expert").astype(jnp.int32)
    slots_dev = w_gate.shape[0] // HB
    rows = slots_dev * CAP
    tok_rows, width = tokens.shape
    half = width // 2
    picks = expert_ids.shape[1]
    packed = jax.ShapeDtypeStruct((2 * rows, half), jnp.bfloat16)
    key = (chip ^ (core * rounds)).reshape(1)

    def travel(arrays):
        return [
            lax.ppermute(
                array,
                ("expert", "tensor"),
                [(2 * i + c, 2 * (i ^ (p + rounds * c)) + c) for i in range(chips) for c in range(2)],
            )
            for p, array in zip(turns(rounds), arrays)
        ]

    pick, *sent = pl.pallas_call(
        functools.partial(pick_kernel, slots_dev),
        out_shape=[jax.ShapeDtypeStruct((picks, 2 * rows * rounds, 2 * tok_rows), jnp.bfloat16)] + [packed] * rounds,
        in_specs=[SMEM, HBM, HBM, HBM],
        out_specs=[VMEM] * (1 + rounds),
        scratch_shapes=[
            pltpu.VMEM((picks, tok_rows), jnp.int32),
            pltpu.VMEM((1, slot_plan.shape[0]), jnp.int32),
            pltpu.VMEM((tok_rows, width), jnp.bfloat16),
            pltpu.SemaphoreType.DMA((3,)),
        ],
        compiler_params=params(16),
        name="pick_rows",
    )(key, *[from_hbm(a) for a in (expert_ids.T, slot_plan.reshape(1, -1), tokens)])

    weights = [w_gate, w_up]
    held = pl.pallas_call(
            fetch_kernel,
            out_shape=[pltpu.VMEM((count, *w_gate.shape[1:]), w_gate.dtype) for count in (w_gate.shape[0], EARLY)],
            in_specs=[ANY] + [HBM] * 2,
            out_specs=[ANY] * 2,
            scratch_shapes=[pltpu.SemaphoreType.DMA((2, 4))],
            compiler_params=params(1),
            cost_estimate=pl.CostEstimate(flops=0, bytes_accessed=2 * 2 * w_gate.size, transcendentals=0),
            name="fetch",
        )(sent[-1], *[from_hbm(w) for w in weights])

    got, held = lax.optimization_barrier((travel(sent), held))
    got = got + [swapped(array, "tensor", 0) for array in got]

    total = chips * rows
    blocks, _, unit = w_gate.shape
    mine, other = pl.pallas_call(
        functools.partial(expert_kernel, slots_dev, chips),
        out_shape=[
            jax.ShapeDtypeStruct((total // 2, width), jnp.float32),
            jax.ShapeDtypeStruct((total // 2, width), jnp.bfloat16),
        ],
        in_specs=[VMEM] * (chips + 2) + [HBM] * 2,
        out_specs=[VMEM] * 2,
        scratch_shapes=[
            pltpu.VMEM((total, width), jnp.bfloat16),
            pltpu.VMEM((blocks, total, unit), jnp.bfloat16),
            pltpu.VMEM((blocks - EARLY, width, unit), jnp.bfloat16),
            pltpu.VMEM((RING, blocks, unit, COLUMNS), jnp.bfloat16),
            pltpu.SemaphoreType.DMA(((blocks - EARLY) // PIECE,)),
            pltpu.SemaphoreType.DMA((width // COLUMNS,)),
        ],
        compiler_params=params(LIMIT),
        name="experts",
    )(*got, *held, from_hbm(w_up), from_hbm(w_down))

    back = pl.pallas_call(
        functools.partial(sum_kernel, rows),
        out_shape=[packed] * rounds,
        in_specs=[VMEM, VMEM],
        out_specs=[VMEM] * rounds,
        compiler_params=params(16),
        name="sum_cores",
    )(mine, swapped(other, "tensor", 0))

    home = travel(back)
    keep, give = pl.pallas_call(
        functools.partial(combine_kernel, rounds),
        out_shape=[
            jax.ShapeDtypeStruct((tok_rows, half), jnp.float32),
            jax.ShapeDtypeStruct((tok_rows, half), jnp.bfloat16),
        ],
        in_specs=[SMEM] + [VMEM] * (2 + rounds),
        out_specs=[VMEM] * 2,
        scratch_shapes=[pltpu.VMEM((2 * tok_rows, half), jnp.float32)],
        compiler_params=params(16),
        name="combine",
    )(core.reshape(1), pick, route_weights.T, *home)
    return (keep + swapped(give, "tensor", 0).astype(jnp.float32)).astype(jnp.bfloat16)


def solution(mesh):
    in_specs = (
        P(("groups", "expert"), None),
        P(("groups", "expert"), None),
        P(("groups", "expert"), None),
        P("groups"),
        P(("groups", "expert"), None, "tensor"),
        P(("groups", "expert"), None, "tensor"),
        P(("groups", "expert"), "tensor", None),
    )
    out_specs = P(("groups", "expert"), "tensor")
    chips = mesh.shape["expert"]
    paired = mesh.shape["tensor"] == 2 and chips in (2, 4, 8) and SLOTS % chips == 0
    body = shards_paired if paired else shards
    return jax.shard_map(body, mesh=mesh, in_specs=in_specs, out_specs=out_specs, check_vma=False)
```

```python
import functools
import jax
import jax.numpy as jnp
import numpy as np
from jax import lax
from jax.experimental import pallas as pl
from jax.experimental.pallas import tpu as pltpu
from jax.sharding import PartitionSpec as P

HB = 4
SLOTS = 32
EXPERTS = 28
CAP = 5
UNROLL = 4
COLUMNS = 896
LIMIT = 26
RING = 3
PIECE = 2
EARLY = 4
MIB = 1 << 20


def swapped(shard, axis, stride):
    return lax.ppermute(shard, axis, [(i, i ^ 1 << stride) for i in range(lax.axis_size(axis))])


def shards(tokens, expert_ids, route_weights, slot_plan, w_gate, w_up, w_down):
    devices = lax.axis_size("expert")
    core = lax.axis_index("tensor")
    blocks_dev = w_gate.shape[0]
    slots_dev = max(1, blocks_dev // HB)
    width = tokens.shape[1]
    half = width // 2
    tok_rows = tokens.shape[0]
    picks_tok = expert_ids.shape[1]
    flat_ids = expert_ids.reshape(-1)
    slot_iota = jnp.arange(SLOTS, dtype=jnp.int32)
    expert_iota = jnp.arange(EXPERTS, dtype=jnp.int32)
    hosted = slot_plan[None, :] == expert_iota[:, None]
    first_slot = jnp.min(jnp.where(hosted, slot_iota[None, :], SLOTS), axis=1)
    naming = (flat_ids[:, None] == expert_iota[None, :]).astype(jnp.int32)
    lowest = jnp.sum(naming * first_slot[None, :], axis=1)
    placed = (lowest[:, None] == slot_iota[None, :]).astype(jnp.int32)
    position = jnp.sum((jnp.cumsum(placed, axis=0) - placed) * placed, axis=1)
    entry_iota = np.arange(devices * slots_dev)
    dest_slot = jnp.asarray(
        entry_iota // slots_dev * blocks_dev // HB + entry_iota % slots_dev, jnp.int32
    )
    slot_match = dest_slot[:, None] == lowest[None, :]
    row_match = jnp.arange(CAP, dtype=jnp.int32)[:, None] == position[None, :]
    routing = (slot_match[:, None, :] & row_match[None, :, :]).astype(jnp.int32)
    routing = routing.reshape(devices * slots_dev * CAP, tok_rows, picks_tok)
    tok_iota = jnp.arange(tok_rows, dtype=jnp.int32)
    source_row = jnp.sum(routing * tok_iota[None, :, None], axis=(1, 2))
    live_row = jnp.sum(routing, axis=(1, 2)) > 0
    block_slot = np.arange(blocks_dev) // HB
    outgoing = jnp.where(live_row[:, None], tokens[source_row], jnp.zeros((), jnp.bfloat16))
    outgoing = outgoing.reshape(devices, slots_dev, CAP, width)
    picked = jnp.take(
        lax.all_to_all(outgoing, "expert", split_axis=0, concat_axis=0, tiled=True),
        block_slot,
        axis=1,
    )
    gate = jnp.einsum("nbcd,bdu->nbcu", picked, w_gate, preferred_element_type=jnp.float32)
    upper = jnp.einsum("nbcd,bdu->nbcu", picked, w_up, preferred_element_type=jnp.float32)
    hidden = (jax.nn.silu(gate) * upper).astype(jnp.bfloat16)
    result = jnp.einsum("nbcu,bud->nbcd", hidden, w_down, preferred_element_type=jnp.float32)
    result = lax.optimization_barrier(result.astype(jnp.bfloat16))
    mine = lax.dynamic_slice_in_dim(result, core * half, half, 3)
    other = lax.dynamic_slice_in_dim(result, (1 - core) * half, half, 3)
    partner = swapped(other, "tensor", 0)
    outputs = (mine.astype(jnp.float32) + partner.astype(jnp.float32)).astype(jnp.bfloat16)
    returned = lax.all_to_all(outputs, "expert", split_axis=0, concat_axis=0, tiled=True)
    returned = returned.reshape(-1, half)
    block_iota = jnp.arange(HB, dtype=jnp.int32)
    row_index = (lowest[:, None] * HB + block_iota[None, :]) * CAP + position[:, None]
    gathered = returned[row_index.reshape(-1)].reshape(tok_rows, picks_tok, HB, half)
    summed = jnp.sum(gathered.astype(jnp.float32), axis=2)
    mixed = jnp.sum(summed * route_weights[:, :, None], axis=1)
    return mixed.astype(jnp.bfloat16)


def quotient(values, divisor):
    return lax.shift_right_logical(values * ((1 << 16) // divisor + 1), 16)


def iota(shape, axis):
    return lax.broadcasted_iota(jnp.int32, shape, axis)


def column(row):
    size = row.shape[1]
    eye = iota((size, size), 0) == iota((size, size), 1)
    return jnp.sum(jnp.where(eye, row, jnp.zeros((), row.dtype)), axis=1, keepdims=True)


def onehot(mask):
    return jnp.where(mask, 1.0, 0.0).astype(jnp.bfloat16)


def dot(left, right, over=1):
    dims = (((over,), (0,)), ((), ()))
    return lax.dot_general(left, right, dims, preferred_element_type=jnp.float32)


def turns(rounds):
    return sorted(range(rounds), key=lambda p: (p < 2, p if p > 1 else -p))


def pick_kernel(slots_dev, key_ref, ids_hbm, plan_hbm, tok_hbm, pick_ref, *refs):
    send_refs, (ids_ref, plan_ref, tok_ref, sems) = refs[:-4], refs[-4:]
    pairs = ((tok_hbm, tok_ref), (ids_hbm, ids_ref), (plan_hbm, plan_ref))
    loads = [pltpu.make_async_copy(a, b, sems.at[i]) for i, (a, b) in enumerate(pairs)]
    for load in loads:
        load.start()
    loads[1].wait()
    loads[2].wait()
    rounds = len(send_refs)
    rows = slots_dev * CAP
    packed = 2 * rows * rounds
    tok_rows, width = tok_ref.shape
    half = width // 2
    slots = plan_ref.shape[1]
    plan = plan_ref[...]
    earlier = (column(plan) == plan) & (iota((slots, slots), 0) < iota((slots, slots), 1))
    repeated = jnp.sum(jnp.where(earlier, 1, 0), axis=0, keepdims=True) > 0
    served = jnp.where(repeated, -1, plan)

    index = iota((packed, 1), 0)
    part = quotient(index, rows)
    entry = quotient(index, CAP)
    rank = index - entry * CAP
    turn = lax.shift_right_logical(part, 1)
    distance = sum(jnp.where(turn == q, p, 0) for q, p in enumerate(turns(rounds)))
    slot = (key_ref[0] ^ distance) * slots_dev + entry - part * slots_dev
    side = part & 1
    chosen = jnp.where(iota((packed, slots), 1) == slot, served, 0)
    expert = jnp.sum(chosen, axis=1, keepdims=True)

    ids = jnp.concatenate([ids_ref[...], ids_ref[...]], axis=1)
    lanes = 2 * tok_rows
    lane = iota((packed, lanes), 1)
    same_side = jnp.where(lane < tok_rows, 0, 1) == side
    named = [(expert == ids[k : k + 1, :]) & same_side for k in range(ids.shape[0])]
    either = functools.reduce(jnp.logical_or, named)
    before = onehot(iota((lanes, lanes), 0) < iota((lanes, lanes), 1))
    in_row = dot(onehot(either), before) == rank.astype(jnp.float32)
    for k, mask in enumerate(named):
        pick_ref[k, :, :] = onehot(mask & in_row)
    loads[0].wait()
    stacked = jnp.concatenate([tok_ref[:, :half], tok_ref[:, half:]], axis=0)
    sent = dot(onehot(either & in_row), stacked).astype(jnp.bfloat16)
    for p, send_ref in enumerate(send_refs):
        send_ref[...] = sent[2 * rows * p : 2 * rows * (p + 1), :]


def fetch_kernel(*refs):
    count = (len(refs) - 2) // 2
    sems = refs[-1]
    pieces = sems.shape[1]
    loads = []
    for a in range(count):
        source, target = refs[1 + a], refs[1 + count + a]
        size = target.shape[0] // pieces
        for i in range(pieces):
            piece = pl.ds(i * size, size)
            loads.append(pltpu.make_async_copy(source.at[piece], target.at[piece], sems.at[a, i]))
    for load in loads:
        load.start()
    for load in loads:
        load.wait()


def expert_kernel(slots_dev, bufs, *refs):
    buf_refs = refs[:bufs]
    gate_ref, up_ref, up_hbm, down_hbm, mine_ref, other_ref = refs[bufs : bufs + 6]
    x_ref, hidden_ref, late_ref, down_ref, late_sems, sems = refs[bufs + 6 :]
    held = up_ref.shape[0]
    ring, blocks, unit, chunk = down_ref.shape
    chunks = down_hbm.shape[2] // chunk
    loads = []
    for i in range(chunks):
        source = down_hbm.at[:, :, pl.ds(i * chunk, chunk)]
        loads.append(pltpu.make_async_copy(source, down_ref.at[i % ring], sems.at[i]))

    def late(i):
        part = pl.ds(i * PIECE, PIECE)
        source = up_hbm.at[pl.ds(held + i * PIECE, PIECE)]
        return pltpu.make_async_copy(source, late_ref.at[part], late_sems.at[i])

    for i in range((blocks - held) // PIECE):
        late(i).start()
    for load in loads[:ring]:
        load.start()
    rows = slots_dev * CAP
    total = bufs * rows
    half = buf_refs[0].shape[1]

    got = jnp.concatenate([ref[...] for ref in buf_refs], axis=0)
    place = iota((total, 2 * total), 0)
    place = place + rows * quotient(place, rows)
    lane = iota((total, 2 * total), 1)
    x_ref[:, :half] = dot(onehot(lane == place), got).astype(jnp.bfloat16)
    x_ref[:, half:] = dot(onehot(lane == place + rows), got).astype(jnp.bfloat16)

    index = iota((total, 1), 0)
    row_slot = quotient(index, CAP) - quotient(index, rows) * slots_dev

    def block(b, up):
        both = dot(x_ref[...], jnp.concatenate([gate_ref[b], up], axis=1))
        gate, upper = both[:, :unit], both[:, unit:]
        value = gate / (1.0 + jnp.exp(-gate)) * upper
        hidden_ref[b] = jnp.where(row_slot == b // HB, value, 0.0).astype(jnp.bfloat16)

    def early_block(b, carry):
        block(b, up_ref[b])
        return carry

    def late_piece(i, carry):
        late(i).wait()
        for j in range(PIECE):
            block(held + i * PIECE + j, late_ref[i * PIECE + j])
        return carry

    lax.fori_loop(0, held, early_block, 0, unroll=min(held, UNROLL))
    lax.fori_loop(0, (blocks - held) // PIECE, late_piece, 0, unroll=3)
    hidden = jnp.concatenate([hidden_ref[b] for b in range(blocks)], axis=1)
    for i in range(chunks):
        cols = slice(i * chunk, (i + 1) * chunk)
        loads[i].wait()
        part = dot(hidden, down_ref[i % ring].reshape(blocks * unit, chunk))
        mine_ref[:, cols] = part[: total // 2, :]
        other_ref[:, cols] = part[total // 2 :, :].astype(jnp.bfloat16)
        if i + ring < chunks:
            loads[i + ring].start()


def sum_kernel(rows, mine_ref, got_ref, *send_refs):
    total = mine_ref.shape[0]
    half = mine_ref.shape[1] // 2
    summed = (mine_ref[...] + got_ref[...].astype(jnp.float32)).astype(jnp.bfloat16)
    stacked = jnp.concatenate([summed[:, :half], summed[:, half:]], axis=0)
    index = iota((2 * total, 2 * total), 0)
    part = quotient(index, rows)
    source = index - rows * part + rows * lax.shift_right_logical(part, 1) + total * (part & 1)
    packed = dot(onehot(iota((2 * total, 2 * total), 1) == source), stacked).astype(jnp.bfloat16)
    for p, send_ref in enumerate(send_refs):
        send_ref[...] = packed[2 * rows * p : 2 * rows * (p + 1), :]


def combine_kernel(bufs, core_ref, pick_ref, weight_ref, *refs):
    got = jnp.concatenate([ref[...] for ref in refs[:bufs]], axis=0)
    keep_ref, give_ref, sum_ref = refs[bufs:]
    tok_rows = keep_ref.shape[0]
    mixed = None
    for k in range(pick_ref.shape[0]):
        weight = column(weight_ref[k : k + 1, :])
        term = dot(pick_ref[k], got, 0) * jnp.concatenate([weight, weight], axis=0)
        mixed = term if mixed is None else mixed + term
    sum_ref[...] = mixed
    core = core_ref[0]
    keep_ref[...] = sum_ref[pl.ds(pl.multiple_of(core * tok_rows, 8), tok_rows), :]
    give_ref[...] = sum_ref[pl.ds(pl.multiple_of((1 - core) * tok_rows, 8), tok_rows), :].astype(jnp.bfloat16)


ANY = pl.BlockSpec(memory_space=pl.ANY)
HBM = pl.BlockSpec(memory_space=pltpu.HBM)
VMEM = pl.BlockSpec(memory_space=pltpu.VMEM)
SMEM = pl.BlockSpec(memory_space=pltpu.SMEM)


def from_hbm(array):
    return pltpu.with_memory_space_constraint(array, pltpu.HBM)


def params(mib):
    return pltpu.CompilerParams(vmem_limit_bytes=mib * MIB)


def shards_paired(tokens, expert_ids, route_weights, slot_plan, w_gate, w_up, w_down):
    chips = lax.axis_size("expert")
    rounds = chips // 2
    core = lax.axis_index("tensor").astype(jnp.int32)
    chip = lax.axis_index("expert").astype(jnp.int32)
    slots_dev = w_gate.shape[0] // HB
    rows = slots_dev * CAP
    tok_rows, width = tokens.shape
    half = width // 2
    picks = expert_ids.shape[1]
    packed = jax.ShapeDtypeStruct((2 * rows, half), jnp.bfloat16)
    key = (chip ^ (core * rounds)).reshape(1)

    def travel(arrays):
        return [
            lax.ppermute(
                array,
                ("expert", "tensor"),
                [(2 * i + c, 2 * (i ^ (p + rounds * c)) + c) for i in range(chips) for c in range(2)],
            )
            for p, array in zip(turns(rounds), arrays)
        ]

    pick, *sent = pl.pallas_call(
        functools.partial(pick_kernel, slots_dev),
        out_shape=[jax.ShapeDtypeStruct((picks, 2 * rows * rounds, 2 * tok_rows), jnp.bfloat16)] + [packed] * rounds,
        in_specs=[SMEM, HBM, HBM, HBM],
        out_specs=[VMEM] * (1 + rounds),
        scratch_shapes=[
            pltpu.VMEM((picks, tok_rows), jnp.int32),
            pltpu.VMEM((1, slot_plan.shape[0]), jnp.int32),
            pltpu.VMEM((tok_rows, width), jnp.bfloat16),
            pltpu.SemaphoreType.DMA((3,)),
        ],
        compiler_params=params(16),
        name="pick_rows",
    )(key, *[from_hbm(a) for a in (expert_ids.T, slot_plan.reshape(1, -1), tokens)])

    weights = [w_gate, w_up]
    held = pl.pallas_call(
            fetch_kernel,
            out_shape=[pltpu.VMEM((count, *w_gate.shape[1:]), w_gate.dtype) for count in (w_gate.shape[0], EARLY)],
            in_specs=[ANY] + [HBM] * 2,
            out_specs=[ANY] * 2,
            scratch_shapes=[pltpu.SemaphoreType.DMA((2, 4))],
            compiler_params=params(1),
            cost_estimate=pl.CostEstimate(flops=0, bytes_accessed=2 * 2 * w_gate.size, transcendentals=0),
            name="fetch",
        )(sent[-1], *[from_hbm(w) for w in weights])

    got, held = lax.optimization_barrier((travel(sent), held))
    got = got + [swapped(array, "tensor", 0) for array in got]

    total = chips * rows
    blocks, _, unit = w_gate.shape
    mine, other = pl.pallas_call(
        functools.partial(expert_kernel, slots_dev, chips),
        out_shape=[
            jax.ShapeDtypeStruct((total // 2, width), jnp.float32),
            jax.ShapeDtypeStruct((total // 2, width), jnp.bfloat16),
        ],
        in_specs=[VMEM] * (chips + 2) + [HBM] * 2,
        out_specs=[VMEM] * 2,
        scratch_shapes=[
            pltpu.VMEM((total, width), jnp.bfloat16),
            pltpu.VMEM((blocks, total, unit), jnp.bfloat16),
            pltpu.VMEM((blocks - EARLY, width, unit), jnp.bfloat16),
            pltpu.VMEM((RING, blocks, unit, COLUMNS), jnp.bfloat16),
            pltpu.SemaphoreType.DMA(((blocks - EARLY) // PIECE,)),
            pltpu.SemaphoreType.DMA((width // COLUMNS,)),
        ],
        compiler_params=params(LIMIT),
        name="experts",
    )(*got, *held, from_hbm(w_up), from_hbm(w_down))

    back = pl.pallas_call(
        functools.partial(sum_kernel, rows),
        out_shape=[packed] * rounds,
        in_specs=[VMEM, VMEM],
        out_specs=[VMEM] * rounds,
        compiler_params=params(16),
        name="sum_cores",
    )(mine, swapped(other, "tensor", 0))

    home = travel(back)
    keep, give = pl.pallas_call(
        functools.partial(combine_kernel, rounds),
        out_shape=[
            jax.ShapeDtypeStruct((tok_rows, half), jnp.float32),
            jax.ShapeDtypeStruct((tok_rows, half), jnp.bfloat16),
        ],
        in_specs=[SMEM] + [VMEM] * (2 + rounds),
        out_specs=[VMEM] * 2,
        scratch_shapes=[pltpu.VMEM((2 * tok_rows, half), jnp.float32)],
        compiler_params=params(16),
        name="combine",
    )(core.reshape(1), pick, route_weights.T, *home)
    return (keep + swapped(give, "tensor", 0).astype(jnp.float32)).astype(jnp.bfloat16)


def solution(mesh):
    in_specs = (
        P(("groups", "expert"), None),
        P(("groups", "expert"), None),
        P(("groups", "expert"), None),
        P("groups"),
        P(("groups", "expert"), None, "tensor"),
        P(("groups", "expert"), None, "tensor"),
        P(("groups", "expert"), "tensor", None),
    )
    out_specs = P(("groups", "expert"), "tensor")
    chips = mesh.shape["expert"]
    paired = mesh.shape["tensor"] == 2 and chips in (2, 4, 8) and SLOTS % chips == 0
    body = shards_paired if paired else shards
    return jax.shard_map(body, mesh=mesh, in_specs=in_specs, out_specs=out_specs, check_vma=False)
```

```python
import functools
import jax
import jax.numpy as jnp
import numpy as np
from jax import lax
from jax.experimental import pallas as pl
from jax.experimental.pallas import tpu as pltpu
from jax.sharding import PartitionSpec as P

HB = 4
SLOTS = 32
EXPERTS = 28
CAP = 5
UNROLL = 4
COLUMNS = 896
LIMIT = 26
RING = 3
PIECE = 2
EARLY = 4
MIB = 1 << 20


def swapped(shard, axis, stride):
    return lax.ppermute(shard, axis, [(i, i ^ 1 << stride) for i in range(lax.axis_size(axis))])


def shards(tokens, expert_ids, route_weights, slot_plan, w_gate, w_up, w_down):
    devices = lax.axis_size("expert")
    core = lax.axis_index("tensor")
    blocks_dev = w_gate.shape[0]
    slots_dev = max(1, blocks_dev // HB)
    width = tokens.shape[1]
    half = width // 2
    tok_rows = tokens.shape[0]
    picks_tok = expert_ids.shape[1]
    flat_ids = expert_ids.reshape(-1)
    slot_iota = jnp.arange(SLOTS, dtype=jnp.int32)
    expert_iota = jnp.arange(EXPERTS, dtype=jnp.int32)
    hosted = slot_plan[None, :] == expert_iota[:, None]
    first_slot = jnp.min(jnp.where(hosted, slot_iota[None, :], SLOTS), axis=1)
    naming = (flat_ids[:, None] == expert_iota[None, :]).astype(jnp.int32)
    lowest = jnp.sum(naming * first_slot[None, :], axis=1)
    placed = (lowest[:, None] == slot_iota[None, :]).astype(jnp.int32)
    position = jnp.sum((jnp.cumsum(placed, axis=0) - placed) * placed, axis=1)
    entry_iota = np.arange(devices * slots_dev)
    dest_slot = jnp.asarray(
        entry_iota // slots_dev * blocks_dev // HB + entry_iota % slots_dev, jnp.int32
    )
    slot_match = dest_slot[:, None] == lowest[None, :]
    row_match = jnp.arange(CAP, dtype=jnp.int32)[:, None] == position[None, :]
    routing = (slot_match[:, None, :] & row_match[None, :, :]).astype(jnp.int32)
    routing = routing.reshape(devices * slots_dev * CAP, tok_rows, picks_tok)
    tok_iota = jnp.arange(tok_rows, dtype=jnp.int32)
    source_row = jnp.sum(routing * tok_iota[None, :, None], axis=(1, 2))
    live_row = jnp.sum(routing, axis=(1, 2)) > 0
    block_slot = np.arange(blocks_dev) // HB
    outgoing = jnp.where(live_row[:, None], tokens[source_row], jnp.zeros((), jnp.bfloat16))
    outgoing = outgoing.reshape(devices, slots_dev, CAP, width)
    picked = jnp.take(
        lax.all_to_all(outgoing, "expert", split_axis=0, concat_axis=0, tiled=True),
        block_slot,
        axis=1,
    )
    gate = jnp.einsum("nbcd,bdu->nbcu", picked, w_gate, preferred_element_type=jnp.float32)
    upper = jnp.einsum("nbcd,bdu->nbcu", picked, w_up, preferred_element_type=jnp.float32)
    hidden = (jax.nn.silu(gate) * upper).astype(jnp.bfloat16)
    result = jnp.einsum("nbcu,bud->nbcd", hidden, w_down, preferred_element_type=jnp.float32)
    result = lax.optimization_barrier(result.astype(jnp.bfloat16))
    mine = lax.dynamic_slice_in_dim(result, core * half, half, 3)
    other = lax.dynamic_slice_in_dim(result, (1 - core) * half, half, 3)
    partner = swapped(other, "tensor", 0)
    outputs = (mine.astype(jnp.float32) + partner.astype(jnp.float32)).astype(jnp.bfloat16)
    returned = lax.all_to_all(outputs, "expert", split_axis=0, concat_axis=0, tiled=True)
    returned = returned.reshape(-1, half)
    block_iota = jnp.arange(HB, dtype=jnp.int32)
    row_index = (lowest[:, None] * HB + block_iota[None, :]) * CAP + position[:, None]
    gathered = returned[row_index.reshape(-1)].reshape(tok_rows, picks_tok, HB, half)
    summed = jnp.sum(gathered.astype(jnp.float32), axis=2)
    mixed = jnp.sum(summed * route_weights[:, :, None], axis=1)
    return mixed.astype(jnp.bfloat16)


def quotient(values, divisor):
    return lax.shift_right_logical(values * ((1 << 16) // divisor + 1), 16)


def iota(shape, axis):
    return lax.broadcasted_iota(jnp.int32, shape, axis)


def column(row):
    size = row.shape[1]
    eye = iota((size, size), 0) == iota((size, size), 1)
    return jnp.sum(jnp.where(eye, row, jnp.zeros((), row.dtype)), axis=1, keepdims=True)


def onehot(mask):
    return jnp.where(mask, 1.0, 0.0).astype(jnp.bfloat16)


def dot(left, right, over=1):
    dims = (((over,), (0,)), ((), ()))
    return lax.dot_general(left, right, dims, preferred_element_type=jnp.float32)


def turns(rounds):
    return sorted(range(rounds), key=lambda p: (p < 2, p if p > 1 else -p))


def pick_kernel(slots_dev, key_ref, ids_hbm, plan_hbm, tok_hbm, pick_ref, *refs):
    send_refs, (ids_ref, plan_ref, tok_ref, sems) = refs[:-4], refs[-4:]
    pairs = ((tok_hbm, tok_ref), (ids_hbm, ids_ref), (plan_hbm, plan_ref))
    loads = [pltpu.make_async_copy(a, b, sems.at[i]) for i, (a, b) in enumerate(pairs)]
    for load in loads:
        load.start()
    loads[1].wait()
    loads[2].wait()
    rounds = len(send_refs)
    rows = slots_dev * CAP
    packed = 2 * rows * rounds
    tok_rows, width = tok_ref.shape
    half = width // 2
    slots = plan_ref.shape[1]
    plan = plan_ref[...]
    earlier = (column(plan) == plan) & (iota((slots, slots), 0) < iota((slots, slots), 1))
    repeated = jnp.sum(jnp.where(earlier, 1, 0), axis=0, keepdims=True) > 0
    served = jnp.where(repeated, -1, plan)

    index = iota((packed, 1), 0)
    part = quotient(index, rows)
    entry = quotient(index, CAP)
    rank = index - entry * CAP
    turn = lax.shift_right_logical(part, 1)
    distance = sum(jnp.where(turn == q, p, 0) for q, p in enumerate(turns(rounds)))
    slot = (key_ref[0] ^ distance) * slots_dev + entry - part * slots_dev
    side = part & 1
    chosen = jnp.where(iota((packed, slots), 1) == slot, served, 0)
    expert = jnp.sum(chosen, axis=1, keepdims=True)

    ids = jnp.concatenate([ids_ref[...], ids_ref[...]], axis=1)
    lanes = 2 * tok_rows
    lane = iota((packed, lanes), 1)
    same_side = jnp.where(lane < tok_rows, 0, 1) == side
    named = [(expert == ids[k : k + 1, :]) & same_side for k in range(ids.shape[0])]
    either = functools.reduce(jnp.logical_or, named)
    before = onehot(iota((lanes, lanes), 0) < iota((lanes, lanes), 1))
    in_row = dot(onehot(either), before) == rank.astype(jnp.float32)
    for k, mask in enumerate(named):
        pick_ref[k, :, :] = onehot(mask & in_row)
    loads[0].wait()
    stacked = jnp.concatenate([tok_ref[:, :half], tok_ref[:, half:]], axis=0)
    sent = dot(onehot(either & in_row), stacked).astype(jnp.bfloat16)
    for p, send_ref in enumerate(send_refs):
        send_ref[...] = sent[2 * rows * p : 2 * rows * (p + 1), :]


def fetch_kernel(*refs):
    count = (len(refs) - 2) // 2
    sems = refs[-1]
    pieces = sems.shape[1]
    loads = []
    for a in range(count):
        source, target = refs[1 + a], refs[1 + count + a]
        size = target.shape[0] // pieces
        for i in range(pieces):
            piece = pl.ds(i * size, size)
            loads.append(pltpu.make_async_copy(source.at[piece], target.at[piece], sems.at[a, i]))
    for load in loads:
        load.start()
    for load in loads:
        load.wait()


def expert_kernel(slots_dev, bufs, *refs):
    buf_refs = refs[:bufs]
    gate_ref, up_ref, up_hbm, down_hbm, mine_ref, other_ref = refs[bufs : bufs + 6]
    x_ref, hidden_ref, late_ref, down_ref, late_sems, sems = refs[bufs + 6 :]
    held = up_ref.shape[0]
    ring, blocks, unit, chunk = down_ref.shape
    chunks = down_hbm.shape[2] // chunk
    loads = []
    for i in range(chunks):
        source = down_hbm.at[:, :, pl.ds(i * chunk, chunk)]
        loads.append(pltpu.make_async_copy(source, down_ref.at[i % ring], sems.at[i]))

    def late(i):
        part = pl.ds(i * PIECE, PIECE)
        source = up_hbm.at[pl.ds(held + i * PIECE, PIECE)]
        return pltpu.make_async_copy(source, late_ref.at[part], late_sems.at[i])

    for i in range((blocks - held) // PIECE):
        late(i).start()
    for load in loads[:ring]:
        load.start()
    rows = slots_dev * CAP
    total = bufs * rows
    half = buf_refs[0].shape[1]

    got = jnp.concatenate([ref[...] for ref in buf_refs], axis=0)
    place = iota((total, 2 * total), 0)
    place = place + rows * quotient(place, rows)
    lane = iota((total, 2 * total), 1)
    x_ref[:, :half] = dot(onehot(lane == place), got).astype(jnp.bfloat16)
    x_ref[:, half:] = dot(onehot(lane == place + rows), got).astype(jnp.bfloat16)

    index = iota((total, 1), 0)
    row_slot = quotient(index, CAP) - quotient(index, rows) * slots_dev

    def block(b, up):
        both = dot(x_ref[...], jnp.concatenate([gate_ref[b], up], axis=1))
        gate, upper = both[:, :unit], both[:, unit:]
        value = gate / (1.0 + jnp.exp(-gate)) * upper
        hidden_ref[b] = jnp.where(row_slot == b // HB, value, 0.0).astype(jnp.bfloat16)

    def early_block(b, carry):
        block(b, up_ref[b])
        return carry

    def late_piece(i, carry):
        late(i).wait()
        for j in range(PIECE):
            block(held + i * PIECE + j, late_ref[i * PIECE + j])
        return carry

    lax.fori_loop(0, held, early_block, 0, unroll=min(held, UNROLL))
    lax.fori_loop(0, (blocks - held) // PIECE, late_piece, 0, unroll=1)
    hidden = jnp.concatenate([hidden_ref[b] for b in range(blocks)], axis=1)
    for i in range(chunks):
        cols = slice(i * chunk, (i + 1) * chunk)
        loads[i].wait()
        part = dot(hidden, down_ref[i % ring].reshape(blocks * unit, chunk))
        mine_ref[:, cols] = part[: total // 2, :]
        other_ref[:, cols] = part[total // 2 :, :].astype(jnp.bfloat16)
        if i + ring < chunks:
            loads[i + ring].start()


def sum_kernel(rows, mine_ref, got_ref, *send_refs):
    total = mine_ref.shape[0]
    half = mine_ref.shape[1] // 2
    summed = (mine_ref[...] + got_ref[...].astype(jnp.float32)).astype(jnp.bfloat16)
    stacked = jnp.concatenate([summed[:, :half], summed[:, half:]], axis=0)
    index = iota((2 * total, 2 * total), 0)
    part = quotient(index, rows)
    source = index - rows * part + rows * lax.shift_right_logical(part, 1) + total * (part & 1)
    packed = dot(onehot(iota((2 * total, 2 * total), 1) == source), stacked).astype(jnp.bfloat16)
    for p, send_ref in enumerate(send_refs):
        send_ref[...] = packed[2 * rows * p : 2 * rows * (p + 1), :]


def combine_kernel(bufs, core_ref, pick_ref, weight_ref, *refs):
    got = jnp.concatenate([ref[...] for ref in refs[:bufs]], axis=0)
    keep_ref, give_ref, sum_ref = refs[bufs:]
    tok_rows = keep_ref.shape[0]
    mixed = None
    for k in range(pick_ref.shape[0]):
        weight = column(weight_ref[k : k + 1, :])
        term = dot(pick_ref[k], got, 0) * jnp.concatenate([weight, weight], axis=0)
        mixed = term if mixed is None else mixed + term
    sum_ref[...] = mixed
    core = core_ref[0]
    keep_ref[...] = sum_ref[pl.ds(pl.multiple_of(core * tok_rows, 8), tok_rows), :]
    give_ref[...] = sum_ref[pl.ds(pl.multiple_of((1 - core) * tok_rows, 8), tok_rows), :].astype(jnp.bfloat16)


ANY = pl.BlockSpec(memory_space=pl.ANY)
HBM = pl.BlockSpec(memory_space=pltpu.HBM)
VMEM = pl.BlockSpec(memory_space=pltpu.VMEM)
SMEM = pl.BlockSpec(memory_space=pltpu.SMEM)


def from_hbm(array):
    return pltpu.with_memory_space_constraint(array, pltpu.HBM)


def params(mib):
    return pltpu.CompilerParams(vmem_limit_bytes=mib * MIB)


def shards_paired(tokens, expert_ids, route_weights, slot_plan, w_gate, w_up, w_down):
    chips = lax.axis_size("expert")
    rounds = chips // 2
    core = lax.axis_index("tensor").astype(jnp.int32)
    chip = lax.axis_index("expert").astype(jnp.int32)
    slots_dev = w_gate.shape[0] // HB
    rows = slots_dev * CAP
    tok_rows, width = tokens.shape
    half = width // 2
    picks = expert_ids.shape[1]
    packed = jax.ShapeDtypeStruct((2 * rows, half), jnp.bfloat16)
    key = (chip ^ (core * rounds)).reshape(1)

    def travel(arrays):
        return [
            lax.ppermute(
                array,
                ("expert", "tensor"),
                [(2 * i + c, 2 * (i ^ (p + rounds * c)) + c) for i in range(chips) for c in range(2)],
            )
            for p, array in zip(turns(rounds), arrays)
        ]

    pick, *sent = pl.pallas_call(
        functools.partial(pick_kernel, slots_dev),
        out_shape=[jax.ShapeDtypeStruct((picks, 2 * rows * rounds, 2 * tok_rows), jnp.bfloat16)] + [packed] * rounds,
        in_specs=[SMEM, HBM, HBM, HBM],
        out_specs=[VMEM] * (1 + rounds),
        scratch_shapes=[
            pltpu.VMEM((picks, tok_rows), jnp.int32),
            pltpu.VMEM((1, slot_plan.shape[0]), jnp.int32),
            pltpu.VMEM((tok_rows, width), jnp.bfloat16),
            pltpu.SemaphoreType.DMA((3,)),
        ],
        compiler_params=params(16),
        name="pick_rows",
    )(key, *[from_hbm(a) for a in (expert_ids.T, slot_plan.reshape(1, -1), tokens)])

    weights = [w_gate, w_up]
    held = pl.pallas_call(
            fetch_kernel,
            out_shape=[pltpu.VMEM((count, *w_gate.shape[1:]), w_gate.dtype) for count in (w_gate.shape[0], EARLY)],
            in_specs=[ANY] + [HBM] * 2,
            out_specs=[ANY] * 2,
            scratch_shapes=[pltpu.SemaphoreType.DMA((2, 4))],
            compiler_params=params(1),
            cost_estimate=pl.CostEstimate(flops=0, bytes_accessed=2 * 2 * w_gate.size, transcendentals=0),
            name="fetch",
        )(sent[-1], *[from_hbm(w) for w in weights])

    got, held = lax.optimization_barrier((travel(sent), held))
    got = got + [swapped(array, "tensor", 0) for array in got]

    total = chips * rows
    blocks, _, unit = w_gate.shape
    mine, other = pl.pallas_call(
        functools.partial(expert_kernel, slots_dev, chips),
        out_shape=[
            jax.ShapeDtypeStruct((total // 2, width), jnp.float32),
            jax.ShapeDtypeStruct((total // 2, width), jnp.bfloat16),
        ],
        in_specs=[VMEM] * (chips + 2) + [HBM] * 2,
        out_specs=[VMEM] * 2,
        scratch_shapes=[
            pltpu.VMEM((total, width), jnp.bfloat16),
            pltpu.VMEM((blocks, total, unit), jnp.bfloat16),
            pltpu.VMEM((blocks - EARLY, width, unit), jnp.bfloat16),
            pltpu.VMEM((RING, blocks, unit, COLUMNS), jnp.bfloat16),
            pltpu.SemaphoreType.DMA(((blocks - EARLY) // PIECE,)),
            pltpu.SemaphoreType.DMA((width // COLUMNS,)),
        ],
        compiler_params=params(LIMIT),
        name="experts",
    )(*got, *held, from_hbm(w_up), from_hbm(w_down))

    back = pl.pallas_call(
        functools.partial(sum_kernel, rows),
        out_shape=[packed] * rounds,
        in_specs=[VMEM, VMEM],
        out_specs=[VMEM] * rounds,
        compiler_params=params(16),
        name="sum_cores",
    )(mine, swapped(other, "tensor", 0))

    home = travel(back)
    keep, give = pl.pallas_call(
        functools.partial(combine_kernel, rounds),
        out_shape=[
            jax.ShapeDtypeStruct((tok_rows, half), jnp.float32),
            jax.ShapeDtypeStruct((tok_rows, half), jnp.bfloat16),
        ],
        in_specs=[SMEM] + [VMEM] * (2 + rounds),
        out_specs=[VMEM] * 2,
        scratch_shapes=[pltpu.VMEM((2 * tok_rows, half), jnp.float32)],
        compiler_params=params(16),
        name="combine",
    )(core.reshape(1), pick, route_weights.T, *home)
    return (keep + swapped(give, "tensor", 0).astype(jnp.float32)).astype(jnp.bfloat16)


def solution(mesh):
    in_specs = (
        P(("groups", "expert"), None),
        P(("groups", "expert"), None),
        P(("groups", "expert"), None),
        P("groups"),
        P(("groups", "expert"), None, "tensor"),
        P(("groups", "expert"), None, "tensor"),
        P(("groups", "expert"), "tensor", None),
    )
    out_specs = P(("groups", "expert"), "tensor")
    chips = mesh.shape["expert"]
    paired = mesh.shape["tensor"] == 2 and chips in (2, 4, 8) and SLOTS % chips == 0
    body = shards_paired if paired else shards
    return jax.shard_map(body, mesh=mesh, in_specs=in_specs, out_specs=out_specs, check_vma=False)
```
